128 devices in a mesh: dom: 8 (over x, core), grp: 16 (over y, z).
Axes of the slice: x: 4, y: 4, z: 4, core: 2. Of those that a mesh axis runs over, the one named last changes fastest.
Arguments:
- features: bfloat16 [524288, 1024], P(('dom', 'grp')), may hold values from -6 to 6
- requests: int32 [128, 128, 13], P(('dom', 'grp')), may hold values from 0 to 4095, as said below
- target_rows: int32 [4096], P(('dom', 'grp')), may hold values from 0 to 4095
- neighbour_slot: int32 [4096, 50], P(('dom', 'grp')), may hold values from 0 to 1663, as said below
- counts: int32 [4096, 50], P(('dom', 'grp')), may hold values from 1 to 63
- hidden_weight: bfloat16 [1024, 2048], P(None, 'grp'), may hold values from -0.1875 to 0.1875
- hidden_bias: float32 [2048], replicated, may hold values from -3 to 3
- output_weight: bfloat16 [3072, 1024], replicated, may hold values from -0.109375 to 0.109375
- output_bias: float32 [1024], replicated, may hold values from -3 to 3
Outputs:
- embedding: bfloat16 [4096, 1024], P(('dom', 'grp'))
The draws below stay inside these ranges and needn't reach their ends.
Inputs may be any that keep to these rules, and one draw needn't show every extreme that they name: `requests`: the rows requested by one device from one owner are distinct; entries at slots that no neighbour names are arbitrary. `neighbour_slot`: the targets of one device name exactly 800 distinct slots; from owner p they are the first c slots p * 13 to p * 13 + c - 1 for some c of 0 to 13, and on every device some owner has all 13 slots named. Several neighbours may share a slot.
All inputs are finite; a program needn't handle non-finite values.
Results may differ from the reference program's by a relative error of at most 0.0065.
Values may be sent and summed in bfloat16 or wider, within the bound.
No kernel may reach another device: no remote copies, remote signals or barrier semaphores. Data moves between devices by JAX's collectives and lax.ppermute only.
A program may use at most 128 MiB of HBM per device.

```python
import jax
import jax.numpy as jnp
from jax import lax

F = 1024
H = 2048
E = 1024
K = 50
TGT_DEV = 32
NODE_DEV = 4096
PEERS = 128
LIVE_DEV = 800
CAP = 13
TARGETS = 4096
NODES = 524288


def owner_counts(key):
    key = jax.random.fold_in(key, 101)
    key_noise, key_order = jax.random.split(key, 2)
    every_slot_index = PEERS * CAP
    random_jitter = jax.random.randint(key_noise, (PEERS, every_slot_index), 0, 32768)
    order_keys = jax.random.split(key_order, PEERS)
    rank_positions = jax.vmap(lambda one_key: jax.random.permutation(one_key, PEERS))(order_keys)
    occupied_flags = max(1, PEERS // 8)
    extra_credit = jnp.where(rank_positions == 0, 262144, jnp.where(rank_positions < occupied_flags, 32768, 0))
    owning_partition = jnp.arange(every_slot_index, dtype=jnp.int32) // CAP
    priority_value = (random_jitter + extra_credit[:, owning_partition]) * every_slot_index + jnp.arange(every_slot_index, dtype=jnp.int32)[None, :]
    chosen = lax.top_k(priority_value, LIVE_DEV)[1]
    marks = jnp.zeros((PEERS, every_slot_index), jnp.int32)
    marks = jax.vmap(lambda row, picks: row.at[picks].set(1))(marks, chosen)
    return jnp.sum(marks.reshape(PEERS, PEERS, CAP), axis=2)


def draw_neighbour_slot(key, part):
    per_owner = owner_counts(key)
    key = jax.random.fold_in(key, 11)
    key_fill, key_order = jax.random.split(key, 2)
    every_slot_index = PEERS * CAP
    live = (jnp.arange(CAP, dtype=jnp.int32)[None, None, :] < per_owner[:, :, None]).reshape(PEERS, every_slot_index)
    live_list = jnp.argsort(jnp.where(live, 0, 1).astype(jnp.int32), axis=1, stable=True)[:, :LIVE_DEV]
    positions = TGT_DEV * K
    extra = jax.random.randint(key_fill, (PEERS, positions), 0, LIVE_DEV)
    index = jnp.where(jnp.arange(positions, dtype=jnp.int32)[None, :] < LIVE_DEV, jnp.arange(positions, dtype=jnp.int32)[None, :], extra)
    slots = jnp.take_along_axis(live_list, index, axis=1)
    order_keys = jax.random.split(key_order, PEERS)
    orders = jax.vmap(lambda one_key: jax.random.permutation(one_key, positions))(order_keys)
    slots = jnp.take_along_axis(slots, orders, axis=1)
    return slots.reshape(PEERS * TGT_DEV, K).astype(jnp.int32)


def draw_requests(key, part):
    key = jax.random.fold_in(key, 23)
    key_start, key_jump = jax.random.split(key, 2)
    start = jax.random.randint(key_start, (PEERS, PEERS, 1), 0, NODE_DEV)
    jump = jax.random.randint(key_jump, (PEERS, PEERS, 1), 1, NODE_DEV // CAP + 1)
    steps = jnp.arange(CAP, dtype=jnp.int32)[None, None, :]
    return ((start + steps * jump) % NODE_DEV).astype(jnp.int32)


def touch_ends(array, own_key, least, top_value):
    longest = array.shape.index(max(array.shape))
    spots = []
    for shift in (0, 1):
        where = [jax.random.randint(jax.random.fold_in(own_key, axis), (), 0, length) for axis, length in enumerate(array.shape)]
        where[longest] = (where[longest] + shift) % array.shape[longest]
        spots.append(tuple(where))
    return array.at[spots[0]].set(least).at[spots[1]].set(top_value)


def steps_of(key, shape, cuts, low, top_value):
    level, own = 1.0, jax.random.fold_in(key, 6)
    for axis_at, shards_of in cuts:
        draws = jnp.exp(jax.random.uniform(jax.random.fold_in(own, axis_at), (shards_of,), jnp.float32, low / len(cuts), top_value / len(cuts)))
        level = level * jnp.repeat(draws, shape[axis_at] // shards_of).reshape([-1 if axis == axis_at else 1 for axis in range(len(shape))])
    return level


def scatter_about(key, dims, deviation, most, cuts=(), kind=jnp.bfloat16):
    loudness = steps_of(key, dims, cuts, -0.22, 0.18) if cuts else 1.0
    drawn = jax.random.normal(key, dims, jnp.float32) * deviation * loudness
    return jnp.minimum(jnp.maximum(drawn, -most), most).astype(kind)


def setup_inputs(seed: int = 0) -> dict:
    streams_of = jax.random.split(jax.random.key(seed), 10)
    return {
        "features": scatter_about(streams_of[0], (NODES, F), 1.0, 6.0, ((0, 128),)),
        "requests": draw_requests(jax.random.fold_in(streams_of[9], 71), 0),
        "target_rows": touch_ends(jax.random.randint(streams_of[2], (TARGETS,), 0, NODE_DEV), jax.random.fold_in(streams_of[2], 1), 0, NODE_DEV - 1).astype(jnp.int32),
        "neighbour_slot": draw_neighbour_slot(jax.random.fold_in(streams_of[9], 71), 0),
        "counts": touch_ends(jax.random.randint(streams_of[4], (TARGETS, K), 1, 64), jax.random.fold_in(streams_of[4], 1), 1, 63).astype(jnp.int32),
        "hidden_weight": scatter_about(streams_of[5], (F, H), F ** -0.5, 0.1875, ((1, 16),)),
        "hidden_bias": scatter_about(streams_of[6], (H,), 0.5, 3.0, (), jnp.float32),
        "output_weight": scatter_about(streams_of[7], (F + H, E), (F + H) ** -0.5, 0.109375),
        "output_bias": scatter_about(streams_of[8], (E,), 0.5, 3.0, (), jnp.float32),
    }


def reference(features, requests, target_rows, neighbour_slot, counts, hidden_weight, hidden_bias, output_weight, output_bias):
    owner_base = (jnp.arange(PEERS, dtype=jnp.int32) * NODE_DEV)[:, None]
    slot_blocks = neighbour_slot.reshape(PEERS, TGT_DEV, K)
    count_blocks = counts.reshape(PEERS, TGT_DEV, K)
    row_blocks = target_rows.reshape(PEERS, TGT_DEV)

    def one_device(items):
        device, wanted, slots, weights, own_rows = items
        node_ids = (owner_base + wanted).reshape(-1)
        picked_nodes = node_ids[slots.reshape(-1)]
        rows = features[picked_nodes]
        transformed = jnp.maximum(jnp.dot(rows, hidden_weight, preferred_element_type=jnp.float32) + hidden_bias, 0.0).astype(jnp.bfloat16)
        transformed = transformed.reshape(TGT_DEV, K, H).astype(jnp.float32)
        weight_f = weights.astype(jnp.float32)
        pooled = lax.optimization_barrier(jnp.sum(weight_f[:, :, None] * transformed, axis=1)) / lax.optimization_barrier(jnp.sum(weight_f, axis=1, keepdims=True))
        pooled = pooled.astype(jnp.bfloat16)
        own = features[device * NODE_DEV + own_rows]
        joined = jnp.concatenate([own, pooled], axis=1)
        combined = jnp.maximum(jnp.dot(joined, output_weight, preferred_element_type=jnp.float32) + output_bias, 0.0)
        scale = lax.rsqrt(lax.optimization_barrier(jnp.mean(combined * combined, axis=1, keepdims=True)) + 1e-06)
        return (combined * scale).astype(jnp.bfloat16)
    devices = jnp.arange(PEERS, dtype=jnp.int32)
    result = lax.map(one_device, (devices, requests, slot_blocks, count_blocks, row_blocks))
    return result.reshape(TARGETS, E)
```

```python
import functools

import jax
import jax.numpy as jnp
from jax import lax
from jax.experimental import pallas as pl
from jax.experimental.pallas import tpu as pltpu
from jax.sharding import PartitionSpec as P

LIVE = 800
LANES = 128
ROWS_AT_ONCE = 256
BLOCK = 256
AXES = ("dom", "grp")
SHIFTS = (0, 1, 3, 2)
GRANT = pltpu.CompilerParams(vmem_limit_bytes=60 * 2**20)


def relayout_kernel(features, rows, held, spread, out, in_sems, out_sems):
    steps = features.shape[0] // ROWS_AT_ONCE
    chunks = features.shape[1] // LANES

    def load(step):
        part = pl.ds(step * ROWS_AT_ONCE, ROWS_AT_ONCE)
        return pltpu.make_async_copy(features.at[part], held.at[part], in_sems.at[step])

    def store(step):
        part = pl.ds(step * ROWS_AT_ONCE, ROWS_AT_ONCE)
        return pltpu.make_async_copy(out.at[part], rows.at[part], out_sems.at[step])

    for step in range(steps):
        load(step).start()
    for step in range(steps):
        load(step).wait()
        part = pl.ds(step * ROWS_AT_ONCE, ROWS_AT_ONCE)
        for chunk in range(chunks):
            piece = held[part, pl.ds(chunk * LANES, LANES)].astype(jnp.float32)
            spread[step % 2, pl.ds(chunk, ROWS_AT_ONCE, stride=chunks), :] = piece
        whole = spread[step % 2].reshape(ROWS_AT_ONCE, chunks, LANES)
        out[part] = whole.astype(jnp.bfloat16)
        store(step).start()
    for step in range(steps):
        store(step).wait()


def relayout(features):
    count, width = features.shape
    chunks = width // LANES
    steps = count // ROWS_AT_ONCE
    hbm = pl.BlockSpec(memory_space=pltpu.HBM)
    return pl.pallas_call(
        relayout_kernel,
        out_shape=jax.ShapeDtypeStruct((count, chunks, LANES), jnp.bfloat16),
        in_specs=[hbm],
        out_specs=hbm,
        scratch_shapes=[
            pltpu.VMEM((count, width), jnp.bfloat16),
            pltpu.VMEM((2, ROWS_AT_ONCE * chunks, LANES), jnp.float32),
            pltpu.VMEM((count, chunks, LANES), jnp.bfloat16),
            pltpu.SemaphoreType.DMA((steps,)),
            pltpu.SemaphoreType.DMA((steps,)),
        ],
        compiler_params=GRANT,
        name="relayout",
    )(features)


def pick_kernel(served, target_rows, rows, outgoing, own, index, own_index, all_rows, held, held_own, sems):
    peers, _, capacity = served.shape
    steps = sems.shape[0] - 4
    span = peers // steps
    first = [
        pltpu.make_async_copy(rows, all_rows, sems.at[steps]),
        pltpu.make_async_copy(served, index, sems.at[steps + 1]),
        pltpu.make_async_copy(target_rows, own_index, sems.at[steps + 2]),
    ]
    for copy in first:
        copy.start()
    for copy in first:
        copy.wait()
    copies = []
    for step in range(steps):

        def peer(p, carry):
            for slot in range(capacity):
                held[p * capacity + slot] = all_rows[index[p, 0, slot]]
            return carry

        lax.fori_loop(step * span, (step + 1) * span, peer, 0)
        part = pl.ds(step * span * capacity, span * capacity)
        copies.append(pltpu.make_async_copy(held.at[part], outgoing.at[part], sems.at[step]))
        copies[-1].start()

    def target(t, carry):
        held_own[t] = all_rows[own_index[t]]
        return carry

    lax.fori_loop(0, own.shape[0], target, 0)
    copies.append(pltpu.make_async_copy(held_own, own, sems.at[steps + 3]))
    copies[-1].start()
    for copy in copies:
        copy.wait()


def pick(served, target_rows, rows):
    peers, _, capacity = served.shape
    tile = rows.shape[1:]
    outgoing = jax.ShapeDtypeStruct((peers * capacity,) + tile, rows.dtype)
    own = jax.ShapeDtypeStruct((target_rows.shape[0],) + tile, rows.dtype)
    hbm = pl.BlockSpec(memory_space=pltpu.HBM)
    anywhere = pl.BlockSpec(memory_space=pl.ANY)
    return pl.pallas_call(
        pick_kernel,
        out_shape=(outgoing, own),
        in_specs=[anywhere, anywhere, hbm],
        out_specs=(hbm, hbm),
        scratch_shapes=[
            pltpu.SMEM(served.shape, jnp.int32),
            pltpu.SMEM(target_rows.shape, jnp.int32),
            pltpu.VMEM(rows.shape, rows.dtype),
            pltpu.VMEM(outgoing.shape, rows.dtype),
            pltpu.VMEM(own.shape, rows.dtype),
            pltpu.SemaphoreType.DMA((8,)),
        ],
        compiler_params=GRANT,
        name="pick",
    )(served, target_rows, rows)


def finish_kernel(
    source, blocks, arrived, own, shares, hidden_bias, output_weight, output_bias, *rest,
):
    mine, other = rest[:4], rest[4:8]
    embedding, spread, live_rows, own_rows, pooled, held_hidden, held_output, sems = rest[8:]
    chunks = arrived.shape[1]
    targets, width = own_rows.shape
    half, side = mine[0].shape[2:]
    copies = []
    for far, parts in enumerate((mine, other)):
        for second, part in enumerate(parts):
            for first in range(part.shape[0]):
                at = 16 * far + 4 * second + first
                rows = pl.ds(pl.multiple_of(blocks[0, at] * half, half), half)
                columns = pl.ds(pl.multiple_of(blocks[1, at] * side, side), side)
                copies.append(
                    pltpu.make_async_copy(part.at[first, 0], held_hidden.at[rows, columns], sems.at[at])
                )
    copies.append(pltpu.make_async_copy(output_weight, held_output, sems.at[32]))
    for copy in copies:
        copy.start()

    def group(g, carry):
        for row in range(16):
            j = g * 16 + row
            place = pl.multiple_of(j * chunks, chunks)
            spread[pl.ds(place, chunks), :] = arrived[source[j]].astype(jnp.float32)
        return carry

    lax.fori_loop(0, LIVE // 16, group, 0)
    for chunk in range(chunks):
        part = spread[pl.ds(chunk, LIVE, stride=chunks), :]
        live_rows[:, pl.ds(chunk * LANES, LANES)] = part.astype(jnp.bfloat16)
    spread[pl.ds(0, targets * chunks), :] = own[...].astype(jnp.float32).reshape(targets * chunks, LANES)
    for chunk in range(chunks):
        part = spread[pl.ds(chunk, targets, stride=chunks), :]
        own_rows[:, pl.ds(chunk * LANES, LANES)] = part.astype(jnp.bfloat16)

    share = shares[...]
    high = jnp.floor(share * (1.0 / 64.0))
    low = share - high * 64.0
    parts = jnp.concatenate([high, low], axis=0).astype(jnp.bfloat16)
    total = jnp.sum(share, axis=1, keepdims=True)
    for copy in copies[:-1]:
        copy.wait()

    def block(n, carry):
        columns = pl.ds(pl.multiple_of(n * BLOCK, BLOCK), BLOCK)
        product = jnp.dot(live_rows[...], held_hidden[:, columns], preferred_element_type=jnp.float32)
        hidden = jnp.maximum(product + hidden_bias[:, columns], 0.0).astype(jnp.bfloat16)
        both = jnp.dot(parts, hidden, preferred_element_type=jnp.float32)
        summed = both[:targets] * 64.0 + both[targets:]
        pooled[:, columns] = (summed / total).astype(jnp.bfloat16)
        return carry

    lax.fori_loop(0, held_hidden.shape[1] // BLOCK, block, 0)
    copies[-1].wait()
    combined = jnp.dot(own_rows[...], held_output[:width], preferred_element_type=jnp.float32)
    combined += jnp.dot(pooled[...], held_output[width:], preferred_element_type=jnp.float32)
    combined = jnp.maximum(combined + output_bias[...], 0.0)
    scale = lax.rsqrt(jnp.mean(combined * combined, axis=1, keepdims=True) + 1e-06)
    embedding[...] = (combined * scale).astype(jnp.bfloat16)


def finish(source, blocks, arrived, own, shares, hidden_bias, output_weight, output_bias, mine, other):
    chunks = arrived.shape[1]
    targets = own.shape[0]
    hidden = hidden_bias.shape[0]
    width = chunks * LANES
    vmem = pl.BlockSpec(memory_space=pltpu.VMEM)
    smem = pl.BlockSpec(memory_space=pltpu.SMEM)
    hbm = pl.BlockSpec(memory_space=pltpu.HBM)
    return pl.pallas_call(
        finish_kernel,
        out_shape=jax.ShapeDtypeStruct((targets, output_weight.shape[1]), jnp.bfloat16),
        in_specs=[smem, smem, vmem, vmem, vmem, vmem, hbm, vmem] + [hbm] * 8,
        out_specs=vmem,
        scratch_shapes=[
            pltpu.VMEM((LIVE * chunks, LANES), jnp.float32),
            pltpu.VMEM((LIVE, width), jnp.bfloat16),
            pltpu.VMEM((targets, width), jnp.bfloat16),
            pltpu.VMEM((targets, hidden), jnp.bfloat16),
            pltpu.VMEM((width, hidden), jnp.bfloat16),
            pltpu.VMEM(output_weight.shape, jnp.bfloat16),
            pltpu.SemaphoreType.DMA((33,)),
        ],
        compiler_params=GRANT,
        name="finish",
    )(
        source, blocks, arrived, own, shares, hidden_bias.reshape(1, -1), output_weight,
        output_bias.reshape(1, -1), *mine, *other,
    )


def plan(neighbour_slot, counts, peers, capacity):
    owner, slot = neighbour_slot // capacity, neighbour_slot % capacity
    same = owner[:, :, None] == jnp.arange(peers, dtype=jnp.int32)
    used = jnp.max(jnp.where(same, slot[:, :, None] + 1, 0), axis=(0, 1))
    before = jnp.arange(peers)[:, None] < jnp.arange(peers)[None, :]
    start = jnp.sum(jnp.where(before, used[:, None], 0), axis=0)
    place = jnp.sum(jnp.where(same, start, 0), axis=2) + slot
    live = jnp.arange(LIVE, dtype=jnp.int32)
    hit = place[:, :, None] == live
    shares = jnp.sum(jnp.where(hit, counts[:, :, None], 0), axis=1).astype(jnp.float32)
    within = (start <= live[:, None]) & (live[:, None] < start + used)
    first = jnp.arange(peers, dtype=jnp.int32) * capacity - start
    source = jnp.sum(jnp.where(within, first, 0), axis=1) + live
    return source, shares


def shifted(x, second, by):
    pairs = []
    for dom in range(8):
        for grp in range(16):
            row, column = grp // 4, grp % 4
            if (dom % 2 == 0) != second:
                row = (row + by) % 4
            else:
                column = (column + by) % 4
            pairs.append((dom * 16 + grp, dom * 16 + row * 4 + column))
    return lax.ppermute(x, AXES, pairs)


def own_half(weight):
    halves = weight.reshape(2, 1, weight.shape[0] // 2, weight.shape[1])
    return jnp.where(lax.axis_index("dom") % 2 == 0, halves[:1], halves[1:])


def block_places():
    core = lax.axis_index("dom") % 2
    row, column = lax.axis_index("grp") // 4, lax.axis_index("grp") % 4
    back = jnp.array(SHIFTS, jnp.int32)
    rows, columns = (row - back) % 4, (column - back) % 4
    of_core0 = (rows[None, :] * 4 + columns[:, None]).reshape(-1)
    of_core1 = (rows[:, None] * 4 + columns[None, :]).reshape(-1)
    same, across = jnp.where(core == 0, of_core0, of_core1), jnp.where(core == 0, of_core1, of_core0)
    half = jnp.repeat(jnp.stack([core, 1 - core]), 16)
    return jnp.stack([half, jnp.concatenate([same, across])]).astype(jnp.int32)


def on_device(
    features,
    requests,
    target_rows,
    neighbour_slot,
    counts,
    hidden_weight,
    hidden_bias,
    output_weight,
    output_bias,
):
    _, peers, capacity = requests.shape
    served = lax.all_to_all(requests.reshape(peers, 1, capacity), AXES, split_axis=0, concat_axis=0, tiled=True)
    own_part = own_half(hidden_weight)
    near = [own_part] + [shifted(own_part, False, by) for by in SHIFTS[1:]]
    rows = relayout(features)
    near = jnp.concatenate(near, axis=0)
    rows, near = lax.optimization_barrier((rows, near))
    mine = [near] + [shifted(near, True, by) for by in SHIFTS[1:]]
    outgoing, own = pick(served, target_rows, rows)
    tile = outgoing.shape[1:]
    blocks = outgoing.reshape(peers, capacity * tile[0], tile[1])
    blocks, neighbour_slot, counts, mine = lax.optimization_barrier((blocks, neighbour_slot, counts, mine))
    arrived = lax.all_to_all(blocks, AXES, split_axis=0, concat_axis=0, tiled=True)
    other = [lax.ppermute(part, "dom", [(dom, dom ^ 1) for dom in range(8)]) for part in mine]
    places = block_places()
    source, shares = plan(neighbour_slot, counts, peers, capacity)
    return finish(
        source, places, arrived.reshape((peers * capacity,) + tile), own, shares, hidden_bias, output_weight,
        output_bias, mine, other,
    )


def solution(mesh):
    placed = (
        P(AXES, None),
        P(AXES, None, None),
        P(AXES),
        P(AXES, None),
        P(AXES, None),
        P(None, "grp"),
        P(),
        P(),
        P(),
    )
    return jax.shard_map(on_device, mesh=mesh, in_specs=placed, out_specs=P(AXES, None), check_vma=False)
```

```python
import functools

import jax
import jax.numpy as jnp
from jax import lax
from jax.experimental import pallas as pl
from jax.experimental.pallas import tpu as pltpu
from jax.sharding import PartitionSpec as P

LIVE = 800
LANES = 128
ROWS_AT_ONCE = 256
BLOCK = 512
AXES = ("dom", "grp")
SHIFTS = (0, 1, 3, 2)
GRANT = pltpu.CompilerParams(vmem_limit_bytes=32 * 2**20)


def takes(microseconds):
    return pl.CostEstimate(flops=int(microseconds * 1.15e9), bytes_accessed=1, transcendentals=0)


def in_hbm(x):
    return pltpu.with_memory_space_constraint(x, pltpu.HBM)


def relayout_kernel(features, rows, held, spread, out, in_sems, out_sems):
    steps = features.shape[0] // ROWS_AT_ONCE
    chunks = features.shape[1] // LANES

    def load(step):
        part = pl.ds(step * ROWS_AT_ONCE, ROWS_AT_ONCE)
        return pltpu.make_async_copy(features.at[part], held.at[part], in_sems.at[step])

    def store(step):
        part = pl.ds(step * ROWS_AT_ONCE, ROWS_AT_ONCE)
        return pltpu.make_async_copy(out.at[part], rows.at[part], out_sems.at[step])

    for step in range(steps):
        load(step).start()
    for step in range(steps):
        load(step).wait()
        part = pl.ds(step * ROWS_AT_ONCE, ROWS_AT_ONCE)
        for chunk in range(chunks):
            piece = held[part, pl.ds(chunk * LANES, LANES)].astype(jnp.float32)
            spread[step % 2, pl.ds(chunk, ROWS_AT_ONCE, stride=chunks), :] = piece
        whole = spread[step % 2].reshape(ROWS_AT_ONCE, chunks, LANES)
        out[part] = whole.astype(jnp.bfloat16)
        store(step).start()
    for step in range(steps):
        store(step).wait()


def relayout(features):
    count, width = features.shape
    chunks = width // LANES
    steps = count // ROWS_AT_ONCE
    hbm = pl.BlockSpec(memory_space=pltpu.HBM)
    return pl.pallas_call(
        relayout_kernel,
        out_shape=pltpu.HBM((count, chunks, LANES), jnp.bfloat16),
        in_specs=[hbm],
        out_specs=hbm,
        scratch_shapes=[
            pltpu.VMEM((count, width), jnp.bfloat16),
            pltpu.VMEM((2, ROWS_AT_ONCE * chunks, LANES), jnp.float32),
            pltpu.VMEM((count, chunks, LANES), jnp.bfloat16),
            pltpu.SemaphoreType.DMA((steps,)),
            pltpu.SemaphoreType.DMA((steps,)),
        ],
        compiler_params=GRANT,
        cost_estimate=takes(7),
        name="relayout",
    )(in_hbm(features))


def pick_kernel(served, target_rows, rows, outgoing, own, index, own_index, all_rows, held, held_own, sems):
    peers, _, capacity = served.shape
    steps = sems.shape[0] - 4
    span = peers // steps
    first = [
        pltpu.make_async_copy(rows, all_rows, sems.at[steps]),
        pltpu.make_async_copy(served, index, sems.at[steps + 1]),
        pltpu.make_async_copy(target_rows, own_index, sems.at[steps + 2]),
    ]
    for copy in first:
        copy.start()
    for copy in first:
        copy.wait()
    copies = []
    for step in range(steps):

        def peer(p, carry):
            for slot in range(capacity):
                held[p * capacity + slot] = all_rows[index[p, 0, slot]]
            return carry

        lax.fori_loop(step * span, (step + 1) * span, peer, 0)
        part = pl.ds(step * span * capacity, span * capacity)
        copies.append(pltpu.make_async_copy(held.at[part], outgoing.at[part], sems.at[step]))
        copies[-1].start()

    def target(t, carry):
        held_own[t] = all_rows[own_index[t]]
        return carry

    lax.fori_loop(0, own.shape[0], target, 0)
    copies.append(pltpu.make_async_copy(held_own, own, sems.at[steps + 3]))
    copies[-1].start()
    for copy in copies:
        copy.wait()


def pick(served, target_rows, rows):
    peers, _, capacity = served.shape
    tile = rows.shape[1:]
    outgoing = pltpu.HBM((peers * capacity,) + tile, rows.dtype)
    own = pltpu.HBM((target_rows.shape[0],) + tile, rows.dtype)
    hbm = pl.BlockSpec(memory_space=pltpu.HBM)
    anywhere = pl.BlockSpec(memory_space=pl.ANY)
    return pl.pallas_call(
        pick_kernel,
        out_shape=(outgoing, own),
        in_specs=[anywhere, anywhere, hbm],
        out_specs=(hbm, hbm),
        scratch_shapes=[
            pltpu.SMEM(served.shape, jnp.int32),
            pltpu.SMEM(target_rows.shape, jnp.int32),
            pltpu.VMEM(rows.shape, rows.dtype),
            pltpu.VMEM((peers * capacity,) + tile, rows.dtype),
            pltpu.VMEM((target_rows.shape[0],) + tile, rows.dtype),
            pltpu.SemaphoreType.DMA((8,)),
        ],
        compiler_params=GRANT,
        cost_estimate=takes(2),
        name="pick",
    )(served, target_rows, in_hbm(rows))


def finish_kernel(
    source, blocks, arrived, own, shares, hidden_bias, output_weight, output_bias, *rest,
):
    mine, other = rest[:4], rest[4:8]
    embedding, spread, live_rows, own_rows, pooled, held_hidden, held_output, sems = rest[8:]
    chunks = arrived.shape[1]
    targets, width = own_rows.shape
    half, side = mine[0].shape[2:]
    copies = []
    for far, parts in enumerate((mine, other)):
        for second, part in enumerate(parts):
            for first in range(part.shape[0]):
                at = 16 * far + 4 * second + first
                rows = pl.ds(pl.multiple_of(blocks[0, at] * half, half), half)
                columns = pl.ds(pl.multiple_of(blocks[1, at] * side, side), side)
                copies.append(
                    pltpu.make_async_copy(part.at[first, 0], held_hidden.at[rows, columns], sems.at[at])
                )
    copies.append(pltpu.make_async_copy(output_weight, held_output, sems.at[32]))
    for copy in copies:
        copy.start()

    def group(g, carry):
        for row in range(16):
            j = g * 16 + row
            place = pl.multiple_of(j * chunks, chunks)
            spread[pl.ds(place, chunks), :] = arrived[source[j]].astype(jnp.float32)
        return carry

    lax.fori_loop(0, LIVE // 16, group, 0)
    for chunk in range(chunks):
        part = spread[pl.ds(chunk, LIVE, stride=chunks), :]
        live_rows[:, pl.ds(chunk * LANES, LANES)] = part.astype(jnp.bfloat16)
    spread[pl.ds(0, targets * chunks), :] = own[...].astype(jnp.float32).reshape(targets * chunks, LANES)
    for chunk in range(chunks):
        part = spread[pl.ds(chunk, targets, stride=chunks), :]
        own_rows[:, pl.ds(chunk * LANES, LANES)] = part.astype(jnp.bfloat16)

    share = shares[...]
    high = jnp.floor(share * (1.0 / 64.0))
    low = share - high * 64.0
    parts = jnp.concatenate([high, low], axis=0).astype(jnp.bfloat16)
    total = jnp.sum(share, axis=1, keepdims=True)
    for copy in copies[:-1]:
        copy.wait()

    def block(n, carry):
        columns = pl.ds(pl.multiple_of(n * BLOCK, BLOCK), BLOCK)
        product = jnp.dot(live_rows[...], held_hidden[:, columns], preferred_element_type=jnp.float32)
        hidden = jnp.maximum(product + hidden_bias[:, columns], 0.0).astype(jnp.bfloat16)
        both = jnp.dot(parts, hidden, preferred_element_type=jnp.float32)
        summed = both[:targets] * 64.0 + both[targets:]
        pooled[:, columns] = (summed / total).astype(jnp.bfloat16)
        return carry

    lax.fori_loop(0, held_hidden.shape[1] // BLOCK, block, 0)
    copies[-1].wait()
    combined = jnp.dot(own_rows[...], held_output[:width], preferred_element_type=jnp.float32)
    combined += jnp.dot(pooled[...], held_output[width:], preferred_element_type=jnp.float32)
    combined = jnp.maximum(combined + output_bias[...], 0.0)
    scale = lax.rsqrt(jnp.mean(combined * combined, axis=1, keepdims=True) + 1e-06)
    embedding[...] = (combined * scale).astype(jnp.bfloat16)


def finish(source, blocks, arrived, own, shares, hidden_bias, output_weight, output_bias, mine, other):
    chunks = arrived.shape[1]
    targets = own.shape[0]
    hidden = hidden_bias.shape[0]
    width = chunks * LANES
    vmem = pl.BlockSpec(memory_space=pltpu.VMEM)
    smem = pl.BlockSpec(memory_space=pltpu.SMEM)
    hbm = pl.BlockSpec(memory_space=pltpu.HBM)
    return pl.pallas_call(
        finish_kernel,
        out_shape=jax.ShapeDtypeStruct((targets, output_weight.shape[1]), jnp.bfloat16),
        in_specs=[smem, smem, vmem, vmem, vmem, vmem, hbm, vmem] + [hbm] * 8,
        out_specs=vmem,
        scratch_shapes=[
            pltpu.VMEM((LIVE * chunks, LANES), jnp.float32),
            pltpu.VMEM((LIVE, width), jnp.bfloat16),
            pltpu.VMEM((targets, width), jnp.bfloat16),
            pltpu.VMEM((targets, hidden), jnp.bfloat16),
            pltpu.VMEM((width, hidden), jnp.bfloat16),
            pltpu.VMEM(output_weight.shape, jnp.bfloat16),
            pltpu.SemaphoreType.DMA((33,)),
        ],
        compiler_params=GRANT,
        name="finish",
    )(
        source, blocks, pltpu.with_memory_space_constraint(arrived, pltpu.VMEM), own, shares,
        hidden_bias.reshape(1, -1), in_hbm(output_weight), output_bias.reshape(1, -1),
        *[in_hbm(part) for part in mine + other],
    )


def plan(neighbour_slot, counts, peers, capacity):
    owner, slot = neighbour_slot // capacity, neighbour_slot % capacity
    same = owner[:, :, None] == jnp.arange(peers, dtype=jnp.int32)
    used = jnp.max(jnp.where(same, slot[:, :, None] + 1, 0), axis=(0, 1))
    before = jnp.arange(peers)[:, None] < jnp.arange(peers)[None, :]
    start = jnp.sum(jnp.where(before, used[:, None], 0), axis=0)
    place = jnp.sum(jnp.where(same, start, 0), axis=2) + slot
    live = jnp.arange(LIVE, dtype=jnp.int32)
    hit = place[:, :, None] == live
    shares = jnp.sum(jnp.where(hit, counts[:, :, None], 0), axis=1).astype(jnp.float32)
    within = (start <= live[:, None]) & (live[:, None] < start + used)
    first = jnp.arange(peers, dtype=jnp.int32) * capacity - start
    source = jnp.sum(jnp.where(within, first, 0), axis=1) + live
    return source, shares


def shifted(x, second, by):
    pairs = []
    for dom in range(8):
        for grp in range(16):
            row, column = grp // 4, grp % 4
            if (dom % 2 == 0) != second:
                row = (row + by) % 4
            else:
                column = (column + by) % 4
            pairs.append((dom * 16 + grp, dom * 16 + row * 4 + column))
    return lax.ppermute(x, AXES, pairs)


def own_half(weight):
    halves = weight.reshape(2, 1, weight.shape[0] // 2, weight.shape[1])
    return jnp.where(lax.axis_index("dom") % 2 == 0, halves[:1], halves[1:])


def block_places():
    core = lax.axis_index("dom") % 2
    row, column = lax.axis_index("grp") // 4, lax.axis_index("grp") % 4
    back = jnp.array(SHIFTS, jnp.int32)
    rows, columns = (row - back) % 4, (column - back) % 4
    of_core0 = (rows[None, :] * 4 + columns[:, None]).reshape(-1)
    of_core1 = (rows[:, None] * 4 + columns[None, :]).reshape(-1)
    same, across = jnp.where(core == 0, of_core0, of_core1), jnp.where(core == 0, of_core1, of_core0)
    half = jnp.repeat(jnp.stack([core, 1 - core]), 16)
    return jnp.stack([half, jnp.concatenate([same, across])]).astype(jnp.int32)


def on_device(
    features,
    requests,
    target_rows,
    neighbour_slot,
    counts,
    hidden_weight,
    hidden_bias,
    output_weight,
    output_bias,
):
    _, peers, capacity = requests.shape
    served = lax.all_to_all(requests.reshape(peers, 1, capacity), AXES, split_axis=0, concat_axis=0, tiled=True)
    own_part = own_half(hidden_weight)
    near = [own_part] + [shifted(own_part, False, by) for by in SHIFTS[1:]]
    rows = relayout(features)
    near = jnp.concatenate(near, axis=0)
    mine = [near] + [shifted(near, True, by) for by in SHIFTS[1:]]
    outgoing, own = pick(served, target_rows, rows)
    tile = outgoing.shape[1:]
    blocks = outgoing.reshape(peers, capacity * tile[0], tile[1])
    blocks, neighbour_slot, counts, mine = lax.optimization_barrier((blocks, neighbour_slot, counts, mine))
    arrived = lax.all_to_all(blocks, AXES, split_axis=0, concat_axis=0, tiled=True)
    other = [lax.ppermute(part, "dom", [(dom, dom ^ 1) for dom in range(8)]) for part in mine]
    places = block_places()
    source, shares = plan(neighbour_slot, counts, peers, capacity)
    return finish(
        source, places, arrived.reshape((peers * capacity,) + tile), own, shares, hidden_bias, output_weight,
        output_bias, mine, other,
    )


def solution(mesh):
    placed = (
        P(AXES, None),
        P(AXES, None, None),
        P(AXES),
        P(AXES, None),
        P(AXES, None),
        P(None, "grp"),
        P(),
        P(),
        P(),
    )
    return jax.shard_map(on_device, mesh=mesh, in_specs=placed, out_specs=P(AXES, None), check_vma=False)
```

```python
import functools

import jax
import jax.numpy as jnp
from jax import lax
from jax.experimental import pallas as pl
from jax.experimental.pallas import tpu as pltpu
from jax.sharding import PartitionSpec as P

LIVE = 800
LANES = 128
ROWS_AT_ONCE = 256
BLOCK = 1024
GROUP = 32
PEERS_AT_ONCE = 4
COST_PICK, COST_PREPARE = 7, 18
AXES = ("dom", "grp")
SHIFTS = (0, 1, 3, 2)
GRANT = pltpu.CompilerParams(vmem_limit_bytes=32 * 2**20)


def takes(microseconds):
    return pl.CostEstimate(flops=int(microseconds * 1.15e9), bytes_accessed=1, transcendentals=0)


def in_hbm(x):
    return pltpu.with_memory_space_constraint(x, pltpu.HBM)


def pick_kernel(
    served, target_rows, features, outgoing, own, index, own_index, held, rows, picked, picked_own, sems, out_sems
):
    peers, _, capacity = served.shape
    loads = features.shape[0] // ROWS_AT_ONCE
    chunks = features.shape[1] // LANES
    stores = out_sems.shape[0] - 1
    span = peers // stores

    def load(step):
        part = pl.ds(step * ROWS_AT_ONCE, ROWS_AT_ONCE)
        return pltpu.make_async_copy(features.at[part], held.at[part], sems.at[step])

    lists = [
        pltpu.make_async_copy(served, index, sems.at[loads]),
        pltpu.make_async_copy(target_rows, own_index, sems.at[loads + 1]),
    ]
    for step in range(loads):
        load(step).start()
    for copy in lists:
        copy.start()
    for step in range(loads):
        load(step).wait()
        part = pl.ds(step * ROWS_AT_ONCE, ROWS_AT_ONCE)
        rows[part] = pltpu.einshape("n(cl)->ncl", held[part, :], c=chunks)
    for copy in lists:
        copy.wait()
    copies = []
    for step in range(stores):

        def some_peers(group, carry):
            for peer in range(PEERS_AT_ONCE):
                for slot in range(capacity):
                    p = group * PEERS_AT_ONCE + peer
                    picked[p * capacity + slot] = rows[index[p, 0, slot]]
            return carry

        groups = span // PEERS_AT_ONCE
        lax.fori_loop(step * groups, (step + 1) * groups, some_peers, 0)
        part = pl.ds(step * span * capacity, span * capacity)
        copies.append(pltpu.make_async_copy(picked.at[part], outgoing.at[part], out_sems.at[step]))
        copies[-1].start()

    def target(t, carry):
        picked_own[t] = rows[own_index[t]]
        return carry

    lax.fori_loop(0, own.shape[0], target, 0)
    copies.append(pltpu.make_async_copy(picked_own, own, out_sems.at[stores]))
    copies[-1].start()
    for copy in copies:
        copy.wait()


def pick(served, target_rows, features):
    peers, _, capacity = served.shape
    count, width = features.shape
    tile = (width // LANES, LANES)
    targets = target_rows.shape[0]
    hbm = pl.BlockSpec(memory_space=pltpu.HBM)
    anywhere = pl.BlockSpec(memory_space=pl.ANY)
    return pl.pallas_call(
        pick_kernel,
        out_shape=(
            pltpu.HBM((peers * capacity,) + tile, features.dtype),
            pltpu.HBM((targets,) + tile, features.dtype),
        ),
        in_specs=[anywhere, anywhere, hbm],
        out_specs=(hbm, hbm),
        scratch_shapes=[
            pltpu.SMEM(served.shape, jnp.int32),
            pltpu.SMEM(target_rows.shape, jnp.int32),
            pltpu.VMEM((count, width), features.dtype),
            pltpu.VMEM((count,) + tile, features.dtype),
            pltpu.VMEM((peers * capacity,) + tile, features.dtype),
            pltpu.VMEM((targets,) + tile, features.dtype),
            pltpu.SemaphoreType.DMA((count // ROWS_AT_ONCE + 2,)),
            pltpu.SemaphoreType.DMA((9,)),
        ],
        compiler_params=GRANT,
        cost_estimate=takes(COST_PICK),
        name="pick",
    )(served, in_hbm(target_rows), in_hbm(features))


def prepare_kernel(
    blocks, own, shares, output_weight, output_bias, *rest,
):
    mine, other = rest[:4], rest[4:8]
    hidden_weight, base, parts, total = rest[8:12]
    whole, spread, own_rows, held, held_base, held_parts, held_total, sems = rest[12:]
    targets, chunks, _ = own.shape
    half, side = mine[0].shape[2:]
    first_rows = pltpu.make_async_copy(output_weight.at[pl.ds(0, held.shape[0])], held, sems.at[32])
    first_rows.start()
    copies = []
    for far, pieces in enumerate((mine, other)):
        for second, piece in enumerate(pieces):
            for first in range(piece.shape[0]):
                at = 16 * far + 4 * second + first
                rows = pl.ds(pl.multiple_of(blocks[0, at] * half, half), half)
                columns = pl.ds(pl.multiple_of(blocks[1, at] * side, side), side)
                copies.append(
                    pltpu.make_async_copy(piece.at[first, 0], whole.at[rows, columns], sems.at[at])
                )
    for copy in copies:
        copy.start()

    spread[...] = own[...].astype(jnp.float32).reshape(targets * chunks, LANES)
    for chunk in range(chunks):
        part = spread[pl.ds(chunk, targets, stride=chunks), :]
        own_rows[:, pl.ds(chunk * LANES, LANES)] = part.astype(jnp.bfloat16)
    share = shares[...]
    high = jnp.floor(share * (1.0 / 64.0))
    low = share - high * 64.0
    held_parts[...] = jnp.concatenate([high, low], axis=0).astype(jnp.bfloat16)
    held_total[...] = jnp.broadcast_to(jnp.sum(share, axis=1, keepdims=True), held_total.shape)
    first_rows.wait()
    held_base[...] = jnp.dot(own_rows[...], held[...], preferred_element_type=jnp.float32) + output_bias[...]
    for copy in copies:
        copy.wait()
    results = ((whole, hidden_weight), (held_base, base), (held_parts, parts), (held_total, total))
    stores = [pltpu.make_async_copy(held, out, sems.at[33 + at]) for at, (held, out) in enumerate(results)]
    for store in stores:
        store.start()
    for store in stores:
        store.wait()


def prepare(blocks, own, shares, output_weight, output_bias, mine, other):
    targets, chunks, _ = own.shape
    width = chunks * LANES
    units = output_weight.shape[1]
    hidden = output_weight.shape[0] - width
    vmem = pl.BlockSpec(memory_space=pltpu.VMEM)
    hbm = pl.BlockSpec(memory_space=pltpu.HBM)
    return pl.pallas_call(
        prepare_kernel,
        out_shape=(
            pltpu.HBM((width, hidden), jnp.bfloat16),
            pltpu.HBM((targets, units), jnp.float32),
            pltpu.HBM((2 * targets, LIVE), jnp.bfloat16),
            pltpu.HBM((targets, LANES), jnp.float32),
        ),
        in_specs=[pl.BlockSpec(memory_space=pltpu.SMEM), vmem, vmem, hbm, vmem] + [hbm] * 8,
        out_specs=(hbm,) * 4,
        scratch_shapes=[
            pltpu.VMEM((width, hidden), jnp.bfloat16),
            pltpu.VMEM((targets * chunks, LANES), jnp.float32),
            pltpu.VMEM((targets, width), jnp.bfloat16),
            pltpu.VMEM((width, units), jnp.bfloat16),
            pltpu.VMEM((targets, units), jnp.float32),
            pltpu.VMEM((2 * targets, LIVE), jnp.bfloat16),
            pltpu.VMEM((targets, LANES), jnp.float32),
            pltpu.SemaphoreType.DMA((37,)),
        ],
        compiler_params=GRANT,
        cost_estimate=takes(COST_PREPARE),
        name="prepare",
    )(
        blocks, own, shares, in_hbm(output_weight), output_bias.reshape(1, -1),
        *[in_hbm(piece) for piece in mine + other],
    )


def finish_kernel(
    source, arrived, parts_hbm, total_hbm, base_hbm, hidden_bias_hbm, hidden_weight, output_weight,
    embedding, spread, live_rows, pooled, held_hidden, held_output, parts, total, base, hidden_bias, sems,
):
    chunks = arrived.shape[1]
    targets, hidden = pooled.shape
    blocks = hidden // BLOCK
    small = ((parts_hbm, parts), (total_hbm, total), (base_hbm, base), (hidden_bias_hbm, hidden_bias))
    loads = []
    for block in range(blocks):
        columns = pl.ds(block * BLOCK, BLOCK)
        loads.append(
            pltpu.make_async_copy(hidden_weight.at[:, columns], held_hidden.at[:, columns], sems.at[block])
        )
        loads[-1].start()
    rest = [pltpu.make_async_copy(x, held, sems.at[blocks + 1 + at]) for at, (x, held) in enumerate(small)]
    for load in rest:
        load.start()

    def group(g, carry):
        at = lax.rem(g, 2) * (GROUP * chunks)
        for row in range(GROUP):
            place = pl.multiple_of(at + row * chunks, chunks)
            spread[pl.ds(place, chunks), :] = arrived[source[g * GROUP + row]].astype(jnp.float32)
        rows = pl.ds(pl.multiple_of(g * GROUP, GROUP), GROUP)
        for chunk in range(chunks):
            part = spread[pl.ds(at + chunk, GROUP, stride=chunks), :]
            live_rows[rows, pl.ds(chunk * LANES, LANES)] = part.astype(jnp.bfloat16)
        return carry

    lax.fori_loop(0, LIVE // GROUP, group, 0)
    skipped = output_weight.shape[0] - hidden
    last_rows = pltpu.make_async_copy(output_weight.at[pl.ds(skipped, hidden)], held_output, sems.at[blocks])
    last_rows.start()
    for load in rest:
        load.wait()
    for block in range(blocks):
        columns = pl.ds(block * BLOCK, BLOCK)
        loads[block].wait()
        product = jnp.dot(live_rows[...], held_hidden[:, columns], preferred_element_type=jnp.float32)
        transformed = jnp.maximum(product + hidden_bias[:, columns], 0.0).astype(jnp.bfloat16)
        both = jnp.dot(parts[...], transformed, preferred_element_type=jnp.float32)
        summed = both[:targets] * 64.0 + both[targets:]
        pooled[:, columns] = (summed / total[:, :1]).astype(jnp.bfloat16)
    last_rows.wait()
    combined = base[...] + jnp.dot(pooled[...], held_output[...], preferred_element_type=jnp.float32)
    combined = jnp.maximum(combined, 0.0)
    scale = lax.rsqrt(jnp.mean(combined * combined, axis=1, keepdims=True) + 1e-06)
    embedding[...] = (combined * scale).astype(jnp.bfloat16)


def finish(source, arrived, parts, total, base, hidden_bias, hidden_weight, output_weight):
    chunks = arrived.shape[1]
    targets = base.shape[0]
    width, hidden = hidden_weight.shape
    units = output_weight.shape[1]
    vmem = pl.BlockSpec(memory_space=pltpu.VMEM)
    smem = pl.BlockSpec(memory_space=pltpu.SMEM)
    hbm = pl.BlockSpec(memory_space=pltpu.HBM)
    return pl.pallas_call(
        finish_kernel,
        out_shape=jax.ShapeDtypeStruct((targets, units), jnp.bfloat16),
        in_specs=[smem, vmem] + [hbm] * 6,
        out_specs=vmem,
        scratch_shapes=[
            pltpu.VMEM((2 * GROUP * chunks, LANES), jnp.float32),
            pltpu.VMEM((LIVE, width), jnp.bfloat16),
            pltpu.VMEM((targets, hidden), jnp.bfloat16),
            pltpu.VMEM((width, hidden), jnp.bfloat16),
            pltpu.VMEM((hidden, units), jnp.bfloat16),
            pltpu.VMEM(parts.shape, jnp.bfloat16),
            pltpu.VMEM(total.shape, jnp.float32),
            pltpu.VMEM(base.shape, jnp.float32),
            pltpu.VMEM((1, hidden), jnp.float32),
            pltpu.SemaphoreType.DMA((hidden // BLOCK + 5,)),
        ],
        compiler_params=GRANT,
        name="finish",
    )(
        source, pltpu.with_memory_space_constraint(arrived, pltpu.VMEM), in_hbm(parts), in_hbm(total),
        in_hbm(base), in_hbm(hidden_bias.reshape(1, -1)), in_hbm(hidden_weight), in_hbm(output_weight),
    )


def plan(neighbour_slot, counts, peers, capacity):
    owner, slot = neighbour_slot // capacity, neighbour_slot % capacity
    same = owner[:, :, None] == jnp.arange(peers, dtype=jnp.int32)
    used = jnp.max(jnp.where(same, slot[:, :, None] + 1, 0), axis=(0, 1))
    before = jnp.arange(peers)[:, None] < jnp.arange(peers)[None, :]
    start = jnp.sum(jnp.where(before, used[:, None], 0), axis=0)
    place = jnp.sum(jnp.where(same, start, 0), axis=2) + slot
    live = jnp.arange(LIVE, dtype=jnp.int32)
    hit = place[:, :, None] == live
    shares = jnp.sum(jnp.where(hit, counts[:, :, None], 0), axis=1).astype(jnp.float32)
    within = (start <= live[:, None]) & (live[:, None] < start + used)
    first = jnp.arange(peers, dtype=jnp.int32) * capacity - start
    source = jnp.sum(jnp.where(within, first, 0), axis=1) + live
    return source, shares


def shifted(x, second, by):
    pairs = []
    for dom in range(8):
        for grp in range(16):
            row, column = grp // 4, grp % 4
            if (dom % 2 == 0) != second:
                row = (row + by) % 4
            else:
                column = (column + by) % 4
            pairs.append((dom * 16 + grp, dom * 16 + row * 4 + column))
    return lax.ppermute(x, AXES, pairs)


def own_half(weight):
    halves = weight.reshape(2, 1, weight.shape[0] // 2, weight.shape[1])
    return jnp.where(lax.axis_index("dom") % 2 == 0, halves[:1], halves[1:])


def block_places(back):
    core = lax.axis_index("dom") % 2
    row, column = lax.axis_index("grp") // 4, lax.axis_index("grp") % 4
    rows, columns = (row - back) % 4, (column - back) % 4
    of_core0 = (rows[None, :] * 4 + columns[:, None]).reshape(-1)
    of_core1 = (rows[:, None] * 4 + columns[None, :]).reshape(-1)
    same, across = jnp.where(core == 0, of_core0, of_core1), jnp.where(core == 0, of_core1, of_core0)
    half = jnp.repeat(jnp.stack([core, 1 - core]), 16)
    return jnp.stack([half, jnp.concatenate([same, across])]).astype(jnp.int32)


def on_device(
    features,
    requests,
    target_rows,
    neighbour_slot,
    counts,
    hidden_weight,
    hidden_bias,
    output_weight,
    output_bias,
):
    _, peers, capacity = requests.shape
    served = lax.all_to_all(requests.reshape(peers, 1, capacity), AXES, split_axis=0, concat_axis=0, tiled=True)
    own_part = own_half(hidden_weight)
    near = [own_part] + [shifted(own_part, False, by) for by in SHIFTS[1:]]
    near = jnp.concatenate(near, axis=0)
    mine = [near] + [shifted(near, True, by) for by in SHIFTS[1:]]
    outgoing, own = pick(served, target_rows, features)
    tile = outgoing.shape[1:]
    blocks = outgoing.reshape(peers, capacity * tile[0], tile[1])
    arrived = lax.all_to_all(blocks, AXES, split_axis=0, concat_axis=0, tiled=True)
    back = jnp.array(SHIFTS, jnp.int32)
    mine, neighbour_slot, counts, back = lax.optimization_barrier((mine, neighbour_slot, counts, back))
    places = block_places(back)
    other = [lax.ppermute(part, "dom", [(dom, dom ^ 1) for dom in range(8)]) for part in mine]
    source, shares = plan(neighbour_slot, counts, peers, capacity)
    weight, base, parts, total = prepare(places, own, shares, output_weight, output_bias, mine, other)
    return finish(
        source, arrived.reshape((peers * capacity,) + tile), parts, total, base, hidden_bias, weight, output_weight
    )


def solution(mesh):
    placed = (
        P(AXES, None),
        P(AXES, None, None),
        P(AXES),
        P(AXES, None),
        P(AXES, None),
        P(None, "grp"),
        P(),
        P(),
        P(),
    )
    return jax.shard_map(on_device, mesh=mesh, in_specs=placed, out_specs=P(AXES, None), check_vma=False)
```

```python
import functools

import jax
import jax.numpy as jnp
from jax import lax
from jax.experimental import pallas as pl
from jax.experimental.pallas import tpu as pltpu
from jax.sharding import PartitionSpec as P

LIVE = 800
LANES = 128
ROWS_AT_ONCE = 256
BLOCK = 1024
GROUP = 32
PEERS_AT_ONCE = 4
COST_PICK, COST_PREPARE = 7, 18
AXES = ("dom", "grp")
SHIFTS = (0, 1, 3, 2)
GRANT = pltpu.CompilerParams(vmem_limit_bytes=32 * 2**20)


def takes(microseconds):
    return pl.CostEstimate(flops=int(microseconds * 1.15e9), bytes_accessed=1, transcendentals=0)


def in_hbm(x):
    return pltpu.with_memory_space_constraint(x, pltpu.HBM)


def pick_kernel(
    served, target_rows, features, outgoing, own, index, own_index, held, rows, picked, picked_own, sems, out_sems
):
    peers, _, capacity = served.shape
    loads = features.shape[0] // ROWS_AT_ONCE
    chunks = features.shape[1] // LANES
    stores = out_sems.shape[0] - 1
    span = peers // stores

    def load(step):
        part = pl.ds(step * ROWS_AT_ONCE, ROWS_AT_ONCE)
        return pltpu.make_async_copy(features.at[part], held.at[part], sems.at[step])

    lists = [
        pltpu.make_async_copy(served, index, sems.at[loads]),
        pltpu.make_async_copy(target_rows, own_index, sems.at[loads + 1]),
    ]
    for step in range(loads):
        load(step).start()
    for copy in lists:
        copy.start()
    for step in range(loads):
        load(step).wait()
        part = pl.ds(step * ROWS_AT_ONCE, ROWS_AT_ONCE)
        rows[part] = pltpu.einshape("n(cl)->ncl", held[part, :], c=chunks)
    for copy in lists:
        copy.wait()
    copies = []
    for step in range(stores):

        def some_peers(group, carry):
            for peer in range(PEERS_AT_ONCE):
                for slot in range(capacity):
                    p = group * PEERS_AT_ONCE + peer
                    picked[p * capacity + slot] = rows[index[p, 0, slot]]
            return carry

        groups = span // PEERS_AT_ONCE
        lax.fori_loop(step * groups, (step + 1) * groups, some_peers, 0)
        part = pl.ds(step * span * capacity, span * capacity)
        copies.append(pltpu.make_async_copy(picked.at[part], outgoing.at[part], out_sems.at[step]))
        copies[-1].start()

    def target(t, carry):
        picked_own[t] = rows[own_index[t]]
        return carry

    lax.fori_loop(0, own.shape[0], target, 0)
    copies.append(pltpu.make_async_copy(picked_own, own, out_sems.at[stores]))
    copies[-1].start()
    for copy in copies:
        copy.wait()


def pick(served, target_rows, features):
    peers, _, capacity = served.shape
    count, width = features.shape
    tile = (width // LANES, LANES)
    targets = target_rows.shape[0]
    hbm = pl.BlockSpec(memory_space=pltpu.HBM)
    anywhere = pl.BlockSpec(memory_space=pl.ANY)
    return pl.pallas_call(
        pick_kernel,
        out_shape=(
            pltpu.HBM((peers * capacity,) + tile, features.dtype),
            pltpu.HBM((targets,) + tile, features.dtype),
        ),
        in_specs=[anywhere, anywhere, hbm],
        out_specs=(hbm, hbm),
        scratch_shapes=[
            pltpu.SMEM(served.shape, jnp.int32),
            pltpu.SMEM(target_rows.shape, jnp.int32),
            pltpu.VMEM((count, width), features.dtype),
            pltpu.VMEM((count,) + tile, features.dtype),
            pltpu.VMEM((peers * capacity,) + tile, features.dtype),
            pltpu.VMEM((targets,) + tile, features.dtype),
            pltpu.SemaphoreType.DMA((count // ROWS_AT_ONCE + 2,)),
            pltpu.SemaphoreType.DMA((9,)),
        ],
        compiler_params=GRANT,
        cost_estimate=takes(COST_PICK),
        name="pick",
    )(served, in_hbm(target_rows), in_hbm(features))


def prepare_kernel(
    blocks, own, shares, output_weight, output_bias, *rest,
):
    mine, other = rest[:4], rest[4:8]
    hidden_weight, base, parts, total = rest[8:12]
    whole, spread, own_rows, held, held_base, held_parts, held_total, sems = rest[12:]
    targets, chunks, _ = own.shape
    half, side = mine[0].shape[2:]
    first_rows = pltpu.make_async_copy(output_weight.at[pl.ds(0, held.shape[0])], held, sems.at[32])
    first_rows.start()
    copies = []
    for far, pieces in enumerate((mine, other)):
        for second, piece in enumerate(pieces):
            for first in range(piece.shape[0]):
                at = 16 * far + 4 * second + first
                rows = pl.ds(pl.multiple_of(blocks[0, at] * half, half), half)
                columns = pl.ds(pl.multiple_of(blocks[1, at] * side, side), side)
                copies.append(
                    pltpu.make_async_copy(piece.at[first, 0], whole.at[rows, columns], sems.at[at])
                )
    for copy in copies:
        copy.start()

    spread[...] = own[...].astype(jnp.float32).reshape(targets * chunks, LANES)
    for chunk in range(chunks):
        part = spread[pl.ds(chunk, targets, stride=chunks), :]
        own_rows[:, pl.ds(chunk * LANES, LANES)] = part.astype(jnp.bfloat16)
    share = shares[...]
    high = jnp.floor(share * (1.0 / 64.0))
    low = share - high * 64.0
    held_parts[...] = jnp.concatenate([high, low], axis=0).astype(jnp.bfloat16)
    held_total[...] = jnp.broadcast_to(jnp.sum(share, axis=1, keepdims=True), held_total.shape)
    first_rows.wait()
    held_base[...] = jnp.dot(own_rows[...], held[...], preferred_element_type=jnp.float32) + output_bias[...]
    for copy in copies:
        copy.wait()
    results = ((whole, hidden_weight), (held_base, base), (held_parts, parts), (held_total, total))
    stores = [pltpu.make_async_copy(held, out, sems.at[33 + at]) for at, (held, out) in enumerate(results)]
    for store in stores:
        store.start()
    for store in stores:
        store.wait()


def prepare(blocks, own, shares, output_weight, output_bias, mine, other):
    targets, chunks, _ = own.shape
    width = chunks * LANES
    units = output_weight.shape[1]
    hidden = output_weight.shape[0] - width
    vmem = pl.BlockSpec(memory_space=pltpu.VMEM)
    hbm = pl.BlockSpec(memory_space=pltpu.HBM)
    return pl.pallas_call(
        prepare_kernel,
        out_shape=(
            pltpu.HBM((width, hidden), jnp.bfloat16),
            pltpu.HBM((targets, units), jnp.float32),
            pltpu.HBM((2 * targets, LIVE), jnp.bfloat16),
            pltpu.HBM((targets, LANES), jnp.float32),
        ),
        in_specs=[pl.BlockSpec(memory_space=pltpu.SMEM), vmem, vmem, hbm, vmem] + [hbm] * 8,
        out_specs=(hbm,) * 4,
        scratch_shapes=[
            pltpu.VMEM((width, hidden), jnp.bfloat16),
            pltpu.VMEM((targets * chunks, LANES), jnp.float32),
            pltpu.VMEM((targets, width), jnp.bfloat16),
            pltpu.VMEM((width, units), jnp.bfloat16),
            pltpu.VMEM((targets, units), jnp.float32),
            pltpu.VMEM((2 * targets, LIVE), jnp.bfloat16),
            pltpu.VMEM((targets, LANES), jnp.float32),
            pltpu.SemaphoreType.DMA((37,)),
        ],
        compiler_params=GRANT,
        cost_estimate=takes(COST_PREPARE),
        name="prepare",
    )(
        blocks, own, shares, in_hbm(output_weight), output_bias.reshape(1, -1),
        *[in_hbm(piece) for piece in mine + other],
    )


def finish_kernel(
    source, arrived, parts_hbm, total_hbm, base_hbm, hidden_bias_hbm, hidden_weight, output_weight,
    embedding, spread, live_rows, pooled, held_hidden, held_output, parts, total, base, hidden_bias, sems,
):
    chunks = arrived.shape[1]
    targets, hidden = pooled.shape
    blocks = hidden // BLOCK
    small = ((parts_hbm, parts), (total_hbm, total), (base_hbm, base), (hidden_bias_hbm, hidden_bias))
    rest = [pltpu.make_async_copy(x, held, sems.at[blocks + 1 + at]) for at, (x, held) in enumerate(small)]
    for load in rest:
        load.start()
    loads = []
    for block in range(blocks):
        columns = pl.ds(block * BLOCK, BLOCK)
        loads.append(
            pltpu.make_async_copy(hidden_weight.at[:, columns], held_hidden.at[:, columns], sems.at[block])
        )
        loads[-1].start()

    def group(g, carry):
        at = lax.rem(g, 2) * (GROUP * chunks)
        for row in range(GROUP):
            place = pl.multiple_of(at + row * chunks, chunks)
            spread[pl.ds(place, chunks), :] = arrived[source[g * GROUP + row]].astype(jnp.float32)
        rows = pl.ds(pl.multiple_of(g * GROUP, GROUP), GROUP)
        for chunk in range(chunks):
            part = spread[pl.ds(at + chunk, GROUP, stride=chunks), :]
            live_rows[rows, pl.ds(chunk * LANES, LANES)] = part.astype(jnp.bfloat16)
        return carry

    lax.fori_loop(0, LIVE // GROUP, group, 0)
    skipped = output_weight.shape[0] - hidden
    last_rows = pltpu.make_async_copy(output_weight.at[pl.ds(skipped, hidden)], held_output, sems.at[blocks])
    last_rows.start()
    for load in rest:
        load.wait()
    for block in range(blocks):
        columns = pl.ds(block * BLOCK, BLOCK)
        loads[block].wait()
        product = jnp.dot(live_rows[...], held_hidden[:, columns], preferred_element_type=jnp.float32)
        transformed = jnp.maximum(product + hidden_bias[:, columns], 0.0).astype(jnp.bfloat16)
        both = jnp.dot(parts[...], transformed, preferred_element_type=jnp.float32)
        summed = both[:targets] * 64.0 + both[targets:]
        pooled[:, columns] = (summed / total[:, :1]).astype(jnp.bfloat16)
    last_rows.wait()
    combined = base[...] + jnp.dot(pooled[...], held_output[...], preferred_element_type=jnp.float32)
    combined = jnp.maximum(combined, 0.0)
    scale = lax.rsqrt(jnp.mean(combined * combined, axis=1, keepdims=True) + 1e-06)
    embedding[...] = (combined * scale).astype(jnp.bfloat16)


def finish(source, arrived, parts, total, base, hidden_bias, hidden_weight, output_weight):
    chunks = arrived.shape[1]
    targets = base.shape[0]
    width, hidden = hidden_weight.shape
    units = output_weight.shape[1]
    vmem = pl.BlockSpec(memory_space=pltpu.VMEM)
    smem = pl.BlockSpec(memory_space=pltpu.SMEM)
    hbm = pl.BlockSpec(memory_space=pltpu.HBM)
    return pl.pallas_call(
        finish_kernel,
        out_shape=jax.ShapeDtypeStruct((targets, units), jnp.bfloat16),
        in_specs=[smem, vmem] + [hbm] * 6,
        out_specs=vmem,
        scratch_shapes=[
            pltpu.VMEM((2 * GROUP * chunks, LANES), jnp.float32),
            pltpu.VMEM((LIVE, width), jnp.bfloat16),
            pltpu.VMEM((targets, hidden), jnp.bfloat16),
            pltpu.VMEM((width, hidden), jnp.bfloat16),
            pltpu.VMEM((hidden, units), jnp.bfloat16),
            pltpu.VMEM(parts.shape, jnp.bfloat16),
            pltpu.VMEM(total.shape, jnp.float32),
            pltpu.VMEM(base.shape, jnp.float32),
            pltpu.VMEM((1, hidden), jnp.float32),
            pltpu.SemaphoreType.DMA((hidden // BLOCK + 5,)),
        ],
        compiler_params=GRANT,
        name="finish",
    )(
        source, pltpu.with_memory_space_constraint(arrived, pltpu.VMEM), in_hbm(parts), in_hbm(total),
        in_hbm(base), in_hbm(hidden_bias.reshape(1, -1)), in_hbm(hidden_weight), in_hbm(output_weight),
    )


def plan(neighbour_slot, counts, peers, capacity):
    owner, slot = neighbour_slot // capacity, neighbour_slot % capacity
    same = owner[:, :, None] == jnp.arange(peers, dtype=jnp.int32)
    used = jnp.max(jnp.where(same, slot[:, :, None] + 1, 0), axis=(0, 1))
    before = jnp.arange(peers)[:, None] < jnp.arange(peers)[None, :]
    start = jnp.sum(jnp.where(before, used[:, None], 0), axis=0)
    place = jnp.sum(jnp.where(same, start, 0), axis=2) + slot
    live = jnp.arange(LIVE, dtype=jnp.int32)
    hit = place[:, :, None] == live
    shares = jnp.sum(jnp.where(hit, counts[:, :, None], 0), axis=1).astype(jnp.float32)
    within = (start <= live[:, None]) & (live[:, None] < start + used)
    first = jnp.arange(peers, dtype=jnp.int32) * capacity - start
    source = jnp.sum(jnp.where(within, first, 0), axis=1) + live
    return source, shares


def shifted(x, second, by):
    pairs = []
    for dom in range(8):
        for grp in range(16):
            row, column = grp // 4, grp % 4
            if (dom % 2 == 0) != second:
                row = (row + by) % 4
            else:
                column = (column + by) % 4
            pairs.append((dom * 16 + grp, dom * 16 + row * 4 + column))
    return lax.ppermute(x, AXES, pairs)


def own_half(weight):
    halves = weight.reshape(2, 1, weight.shape[0] // 2, weight.shape[1])
    return jnp.where(lax.axis_index("dom") % 2 == 0, halves[:1], halves[1:])


def block_places(back):
    core = lax.axis_index("dom") % 2
    row, column = lax.axis_index("grp") // 4, lax.axis_index("grp") % 4
    rows, columns = (row - back) % 4, (column - back) % 4
    of_core0 = (rows[None, :] * 4 + columns[:, None]).reshape(-1)
    of_core1 = (rows[:, None] * 4 + columns[None, :]).reshape(-1)
    same, across = jnp.where(core == 0, of_core0, of_core1), jnp.where(core == 0, of_core1, of_core0)
    half = jnp.repeat(jnp.stack([core, 1 - core]), 16)
    return jnp.stack([half, jnp.concatenate([same, across])]).astype(jnp.int32)


def on_device(
    features,
    requests,
    target_rows,
    neighbour_slot,
    counts,
    hidden_weight,
    hidden_bias,
    output_weight,
    output_bias,
):
    _, peers, capacity = requests.shape
    served = lax.all_to_all(requests.reshape(peers, 1, capacity), AXES, split_axis=0, concat_axis=0, tiled=True)
    own_part = own_half(hidden_weight)
    near = [own_part] + [shifted(own_part, False, by) for by in SHIFTS[1:]]
    near = jnp.concatenate(near, axis=0)
    mine = [near] + [shifted(near, True, by) for by in SHIFTS[1:]]
    outgoing, own = pick(served, target_rows, features)
    tile = outgoing.shape[1:]
    blocks = outgoing.reshape(peers, capacity * tile[0], tile[1])
    arrived = lax.all_to_all(blocks, AXES, split_axis=0, concat_axis=0, tiled=True)
    back = jnp.array(SHIFTS, jnp.int32)
    mine, neighbour_slot, counts, back = lax.optimization_barrier((mine, neighbour_slot, counts, back))
    places = block_places(back)
    other = [lax.ppermute(part, "dom", [(dom, dom ^ 1) for dom in range(8)]) for part in mine]
    source, shares = plan(neighbour_slot, counts, peers, capacity)
    weight, base, parts, total = prepare(places, own, shares, output_weight, output_bias, mine, other)
    return finish(
        source, arrived.reshape((peers * capacity,) + tile), parts, total, base, hidden_bias, weight, output_weight
    )


def solution(mesh):
    placed = (
        P(AXES, None),
        P(AXES, None, None),
        P(AXES),
        P(AXES, None),
        P(AXES, None),
        P(None, "grp"),
        P(),
        P(),
        P(),
    )
    return jax.shard_map(on_device, mesh=mesh, in_specs=placed, out_specs=P(AXES, None), check_vma=False)
```

```python
import functools

import jax
import jax.numpy as jnp
from jax import lax
from jax.experimental import pallas as pl
from jax.experimental.pallas import tpu as pltpu
from jax.sharding import PartitionSpec as P

LIVE = 800
LANES = 128
ROWS_AT_ONCE = 256
BLOCK = 1024
GROUP = 32
PEERS_AT_ONCE = 4
COST_PICK, COST_PREPARE = 7, 18
AXES = ("dom", "grp")
SHIFTS = (0, 1, 3, 2)
GRANT = pltpu.CompilerParams(vmem_limit_bytes=32 * 2**20)


def takes(microseconds):
    return pl.CostEstimate(flops=int(microseconds * 1.15e9), bytes_accessed=1, transcendentals=0)


def in_hbm(x):
    return pltpu.with_memory_space_constraint(x, pltpu.HBM)


def pick_kernel(
    served, target_rows, features, outgoing, own, index, own_index, held, rows, picked, picked_own, sems, out_sems
):
    peers, _, capacity = served.shape
    loads = features.shape[0] // ROWS_AT_ONCE
    chunks = features.shape[1] // LANES
    stores = out_sems.shape[0] - 1
    span = peers // stores

    def load(step):
        part = pl.ds(step * ROWS_AT_ONCE, ROWS_AT_ONCE)
        return pltpu.make_async_copy(features.at[part], held.at[part], sems.at[step])

    lists = [
        pltpu.make_async_copy(served, index, sems.at[loads]),
        pltpu.make_async_copy(target_rows, own_index, sems.at[loads + 1]),
    ]
    for step in range(loads):
        load(step).start()
    for copy in lists:
        copy.start()
    for step in range(loads):
        load(step).wait()
        part = pl.ds(step * ROWS_AT_ONCE, ROWS_AT_ONCE)
        rows[part] = pltpu.einshape("n(cl)->ncl", held[part, :], c=chunks)
    for copy in lists:
        copy.wait()
    copies = []
    for step in range(stores):

        def some_peers(group, carry):
            for peer in range(PEERS_AT_ONCE):
                for slot in range(capacity):
                    p = group * PEERS_AT_ONCE + peer
                    picked[p * capacity + slot] = rows[index[p, 0, slot]]
            return carry

        groups = span // PEERS_AT_ONCE
        lax.fori_loop(step * groups, (step + 1) * groups, some_peers, 0)
        part = pl.ds(step * span * capacity, span * capacity)
        copies.append(pltpu.make_async_copy(picked.at[part], outgoing.at[part], out_sems.at[step]))
        copies[-1].start()

    def target(t, carry):
        picked_own[t] = rows[own_index[t]]
        return carry

    lax.fori_loop(0, own.shape[0], target, 0)
    copies.append(pltpu.make_async_copy(picked_own, own, out_sems.at[stores]))
    copies[-1].start()
    for copy in copies:
        copy.wait()


def pick(served, target_rows, features):
    peers, _, capacity = served.shape
    count, width = features.shape
    tile = (width // LANES, LANES)
    targets = target_rows.shape[0]
    hbm = pl.BlockSpec(memory_space=pltpu.HBM)
    anywhere = pl.BlockSpec(memory_space=pl.ANY)
    return pl.pallas_call(
        pick_kernel,
        out_shape=(
            pltpu.HBM((peers * capacity,) + tile, features.dtype),
            pltpu.HBM((targets,) + tile, features.dtype),
        ),
        in_specs=[anywhere, anywhere, hbm],
        out_specs=(hbm, hbm),
        scratch_shapes=[
            pltpu.SMEM(served.shape, jnp.int32),
            pltpu.SMEM(target_rows.shape, jnp.int32),
            pltpu.VMEM((count, width), features.dtype),
            pltpu.VMEM((count,) + tile, features.dtype),
            pltpu.VMEM((peers * capacity,) + tile, features.dtype),
            pltpu.VMEM((targets,) + tile, features.dtype),
            pltpu.SemaphoreType.DMA((count // ROWS_AT_ONCE + 2,)),
            pltpu.SemaphoreType.DMA((9,)),
        ],
        compiler_params=GRANT,
        cost_estimate=takes(COST_PICK),
        name="pick",
    )(served, in_hbm(target_rows), in_hbm(features))


def prepare_kernel(
    blocks, own, shares, output_weight, output_bias, *rest,
):
    mine, other = rest[:4], rest[4:8]
    hidden_weight, base, parts, total = rest[8:12]
    whole, spread, own_rows, held, held_base, held_parts, held_total, sems = rest[12:]
    targets, chunks, _ = own.shape
    half, side = mine[0].shape[2:]
    first_rows = pltpu.make_async_copy(output_weight.at[pl.ds(0, held.shape[0])], held, sems.at[32])
    first_rows.start()
    copies = []
    for far, pieces in enumerate((mine, other)):
        for second, piece in enumerate(pieces):
            for first in range(piece.shape[0]):
                at = 16 * far + 4 * second + first
                rows = pl.ds(pl.multiple_of(blocks[0, at] * half, half), half)
                columns = pl.ds(pl.multiple_of(blocks[1, at] * side, side), side)
                copies.append(
                    pltpu.make_async_copy(piece.at[first, 0], whole.at[rows, columns], sems.at[at])
                )
    for copy in copies:
        copy.start()

    spread[...] = own[...].astype(jnp.float32).reshape(targets * chunks, LANES)
    for chunk in range(chunks):
        part = spread[pl.ds(chunk, targets, stride=chunks), :]
        own_rows[:, pl.ds(chunk * LANES, LANES)] = part.astype(jnp.bfloat16)
    share = shares[...]
    high = jnp.floor(share * (1.0 / 64.0))
    low = share - high * 64.0
    held_parts[...] = jnp.concatenate([high, low], axis=0).astype(jnp.bfloat16)
    held_total[...] = jnp.broadcast_to(jnp.sum(share, axis=1, keepdims=True), held_total.shape)
    first_rows.wait()
    held_base[...] = jnp.dot(own_rows[...], held[...], preferred_element_type=jnp.float32) + output_bias[...]
    for copy in copies:
        copy.wait()
    results = ((whole, hidden_weight), (held_base, base), (held_parts, parts), (held_total, total))
    stores = [pltpu.make_async_copy(held, out, sems.at[33 + at]) for at, (held, out) in enumerate(results)]
    for store in stores:
        store.start()
    for store in stores:
        store.wait()


def prepare(blocks, own, shares, output_weight, output_bias, mine, other):
    targets, chunks, _ = own.shape
    width = chunks * LANES
    units = output_weight.shape[1]
    hidden = output_weight.shape[0] - width
    vmem = pl.BlockSpec(memory_space=pltpu.VMEM)
    hbm = pl.BlockSpec(memory_space=pltpu.HBM)
    return pl.pallas_call(
        prepare_kernel,
        out_shape=(
            pltpu.HBM((width, hidden), jnp.bfloat16),
            pltpu.HBM((targets, units), jnp.float32),
            pltpu.HBM((2 * targets, LIVE), jnp.bfloat16),
            pltpu.HBM((targets, LANES), jnp.float32),
        ),
        in_specs=[pl.BlockSpec(memory_space=pltpu.SMEM), vmem, vmem, hbm, vmem] + [hbm] * 8,
        out_specs=(hbm,) * 4,
        scratch_shapes=[
            pltpu.VMEM((width, hidden), jnp.bfloat16),
            pltpu.VMEM((targets * chunks, LANES), jnp.float32),
            pltpu.VMEM((targets, width), jnp.bfloat16),
            pltpu.VMEM((width, units), jnp.bfloat16),
            pltpu.VMEM((targets, units), jnp.float32),
            pltpu.VMEM((2 * targets, LIVE), jnp.bfloat16),
            pltpu.VMEM((targets, LANES), jnp.float32),
            pltpu.SemaphoreType.DMA((37,)),
        ],
        compiler_params=GRANT,
        cost_estimate=takes(COST_PREPARE),
        name="prepare",
    )(
        blocks, own, shares, in_hbm(output_weight), output_bias.reshape(1, -1),
        *[in_hbm(piece) for piece in mine + other],
    )


def finish_kernel(
    source_hbm, arrived, parts_hbm, total_hbm, base_hbm, hidden_bias_hbm, hidden_weight, output_weight,
    embedding, source, spread, live_rows, pooled, held_hidden, held_output, parts, total, base, hidden_bias, sems,
):
    chunks = arrived.shape[1]
    targets, hidden = pooled.shape
    blocks = hidden // BLOCK
    small = ((parts_hbm, parts), (total_hbm, total), (base_hbm, base), (hidden_bias_hbm, hidden_bias))
    slots = pltpu.make_async_copy(source_hbm, source, sems.at[blocks + 5])
    slots.start()
    rest = [pltpu.make_async_copy(x, held, sems.at[blocks + 1 + at]) for at, (x, held) in enumerate(small)]
    for load in rest:
        load.start()
    loads = []
    for block in range(blocks):
        columns = pl.ds(block * BLOCK, BLOCK)
        loads.append(
            pltpu.make_async_copy(hidden_weight.at[:, columns], held_hidden.at[:, columns], sems.at[block])
        )
        loads[-1].start()

    def group(g, carry):
        at = lax.rem(g, 2) * (GROUP * chunks)
        for row in range(GROUP):
            place = pl.multiple_of(at + row * chunks, chunks)
            spread[pl.ds(place, chunks), :] = arrived[source[g * GROUP + row]].astype(jnp.float32)
        rows = pl.ds(pl.multiple_of(g * GROUP, GROUP), GROUP)
        for chunk in range(chunks):
            part = spread[pl.ds(at + chunk, GROUP, stride=chunks), :]
            live_rows[rows, pl.ds(chunk * LANES, LANES)] = part.astype(jnp.bfloat16)
        return carry

    slots.wait()
    lax.fori_loop(0, LIVE // GROUP, group, 0)
    skipped = output_weight.shape[0] - hidden
    last_rows = pltpu.make_async_copy(output_weight.at[pl.ds(skipped, hidden)], held_output, sems.at[blocks])
    last_rows.start()
    for load in rest:
        load.wait()
    for block in range(blocks):
        columns = pl.ds(block * BLOCK, BLOCK)
        loads[block].wait()
        product = jnp.dot(live_rows[...], held_hidden[:, columns], preferred_element_type=jnp.float32)
        transformed = jnp.maximum(product + hidden_bias[:, columns], 0.0).astype(jnp.bfloat16)
        both = jnp.dot(parts[...], transformed, preferred_element_type=jnp.float32)
        summed = both[:targets] * 64.0 + both[targets:]
        pooled[:, columns] = (summed / total[:, :1]).astype(jnp.bfloat16)
    last_rows.wait()
    combined = base[...] + jnp.dot(pooled[...], held_output[...], preferred_element_type=jnp.float32)
    combined = jnp.maximum(combined, 0.0)
    scale = lax.rsqrt(jnp.mean(combined * combined, axis=1, keepdims=True) + 1e-06)
    embedding[...] = (combined * scale).astype(jnp.bfloat16)


def finish(source, arrived, parts, total, base, hidden_bias, hidden_weight, output_weight):
    chunks = arrived.shape[1]
    targets = base.shape[0]
    width, hidden = hidden_weight.shape
    units = output_weight.shape[1]
    vmem = pl.BlockSpec(memory_space=pltpu.VMEM)
    hbm = pl.BlockSpec(memory_space=pltpu.HBM)
    return pl.pallas_call(
        finish_kernel,
        out_shape=jax.ShapeDtypeStruct((targets, units), jnp.bfloat16),
        in_specs=[hbm, vmem] + [hbm] * 6,
        out_specs=vmem,
        scratch_shapes=[
            pltpu.SMEM(source.shape, jnp.int32),
            pltpu.VMEM((2 * GROUP * chunks, LANES), jnp.float32),
            pltpu.VMEM((LIVE, width), jnp.bfloat16),
            pltpu.VMEM((targets, hidden), jnp.bfloat16),
            pltpu.VMEM((width, hidden), jnp.bfloat16),
            pltpu.VMEM((hidden, units), jnp.bfloat16),
            pltpu.VMEM(parts.shape, jnp.bfloat16),
            pltpu.VMEM(total.shape, jnp.float32),
            pltpu.VMEM(base.shape, jnp.float32),
            pltpu.VMEM((1, hidden), jnp.float32),
            pltpu.SemaphoreType.DMA((hidden // BLOCK + 6,)),
        ],
        compiler_params=GRANT,
        name="finish",
    )(
        in_hbm(source), pltpu.with_memory_space_constraint(arrived, pltpu.VMEM), in_hbm(parts), in_hbm(total),
        in_hbm(base), in_hbm(hidden_bias.reshape(1, -1)), in_hbm(hidden_weight), in_hbm(output_weight),
    )


def plan(neighbour_slot, counts, peers, capacity):
    owner, slot = neighbour_slot // capacity, neighbour_slot % capacity
    same = owner[:, :, None] == jnp.arange(peers, dtype=jnp.int32)
    used = jnp.max(jnp.where(same, slot[:, :, None] + 1, 0), axis=(0, 1))
    before = jnp.arange(peers)[:, None] < jnp.arange(peers)[None, :]
    start = jnp.sum(jnp.where(before, used[:, None], 0), axis=0)
    place = jnp.sum(jnp.where(same, start, 0), axis=2) + slot
    live = jnp.arange(LIVE, dtype=jnp.int32)
    hit = place[:, :, None] == live
    shares = jnp.sum(jnp.where(hit, counts[:, :, None], 0), axis=1).astype(jnp.float32)
    within = (start <= live[:, None]) & (live[:, None] < start + used)
    first = jnp.arange(peers, dtype=jnp.int32) * capacity - start
    source = jnp.sum(jnp.where(within, first, 0), axis=1) + live
    return source, shares


def shifted(x, second, by):
    pairs = []
    for dom in range(8):
        for grp in range(16):
            row, column = grp // 4, grp % 4
            if (dom % 2 == 0) != second:
                row = (row + by) % 4
            else:
                column = (column + by) % 4
            pairs.append((dom * 16 + grp, dom * 16 + row * 4 + column))
    return lax.ppermute(x, AXES, pairs)


def join_kernel(*refs):
    weights, (out, held, sems) = refs[:-3], refs[-3:]
    half = out.shape[2]
    core = lax.rem(lax.axis_index("dom"), 2)
    rows = pl.ds(pl.multiple_of(core * half, half), half)
    copies = [pltpu.make_async_copy(x.at[rows], held.at[at, 0], sems.at[at]) for at, x in enumerate(weights)]
    for copy in copies:
        copy.start()
    for copy in copies:
        copy.wait()
    whole = pltpu.make_async_copy(held, out, sems.at[len(weights)])
    whole.start()
    whole.wait()


def join(weights):
    rows, columns = weights[0].shape
    return pl.pallas_call(
        join_kernel,
        out_shape=pltpu.HBM((len(weights), 1, rows // 2, columns), weights[0].dtype),
        in_specs=[pl.BlockSpec(memory_space=pl.ANY)] * len(weights),
        out_specs=pl.BlockSpec(memory_space=pltpu.HBM),
        scratch_shapes=[
            pltpu.VMEM((len(weights), 1, rows // 2, columns), weights[0].dtype),
            pltpu.SemaphoreType.DMA((len(weights) + 1,)),
        ],
        compiler_params=pltpu.CompilerParams(vmem_limit_bytes=4 * 2**20),
        cost_estimate=takes(1),
        name="join",
    )(in_hbm(weights[0]), *weights[1:])


def block_places(back):
    core = lax.axis_index("dom") % 2 + back[0]
    row, column = lax.axis_index("grp") // 4, lax.axis_index("grp") % 4
    rows, columns = (row - back) % 4, (column - back) % 4
    of_core0 = (rows[None, :] * 4 + columns[:, None]).reshape(-1)
    of_core1 = (rows[:, None] * 4 + columns[None, :]).reshape(-1)
    same, across = jnp.where(core == 0, of_core0, of_core1), jnp.where(core == 0, of_core1, of_core0)
    half = jnp.repeat(jnp.stack([core, 1 - core]), 16)
    return jnp.stack([half, jnp.concatenate([same, across])]).astype(jnp.int32)


def on_device(
    features,
    requests,
    target_rows,
    neighbour_slot,
    counts,
    hidden_weight,
    hidden_bias,
    output_weight,
    output_bias,
):
    _, peers, capacity = requests.shape
    served = lax.all_to_all(requests.reshape(peers, 1, capacity), AXES, split_axis=0, concat_axis=0, tiled=True)
    near = join([hidden_weight] + [shifted(hidden_weight, False, by) for by in SHIFTS[1:]])
    mine = [near] + [shifted(near, True, by) for by in SHIFTS[1:]]
    outgoing, own = pick(served, target_rows, features)
    tile = outgoing.shape[1:]
    blocks = outgoing.reshape(peers, capacity * tile[0], tile[1])
    arrived = lax.all_to_all(blocks, AXES, split_axis=0, concat_axis=0, tiled=True)
    back = jnp.array(SHIFTS, jnp.int32)
    mine, neighbour_slot, counts, back = lax.optimization_barrier((mine, neighbour_slot, counts, back))
    places = block_places(back)
    other = [lax.ppermute(part, "dom", [(dom, dom ^ 1) for dom in range(8)]) for part in mine]
    source, shares = plan(neighbour_slot, counts, peers, capacity)
    weight, base, parts, total = prepare(places, own, shares, output_weight, output_bias, mine, other)
    return finish(
        source, arrived.reshape((peers * capacity,) + tile), parts, total, base, hidden_bias, weight, output_weight
    )


def solution(mesh):
    placed = (
        P(AXES, None),
        P(AXES, None, None),
        P(AXES),
        P(AXES, None),
        P(AXES, None),
        P(None, "grp"),
        P(),
        P(),
        P(),
    )
    return jax.shard_map(on_device, mesh=mesh, in_specs=placed, out_specs=P(AXES, None), check_vma=False)
```

```python
import functools

import jax
import jax.numpy as jnp
from jax import lax
from jax.experimental import pallas as pl
from jax.experimental.pallas import tpu as pltpu
from jax.sharding import PartitionSpec as P

LIVE = 800
LANES = 128
ROWS_AT_ONCE = 256
BLOCK = 1024
GROUP = 32
PEERS_AT_ONCE = 4
COST_PICK, COST_PREPARE = 7, 18
AXES = ("dom", "grp")
SHIFTS = (0, 1, 3, 2)
GRANT = pltpu.CompilerParams(vmem_limit_bytes=32 * 2**20)


def takes(microseconds):
    return pl.CostEstimate(flops=int(microseconds * 1.15e9), bytes_accessed=1, transcendentals=0)


def in_hbm(x):
    return pltpu.with_memory_space_constraint(x, pltpu.HBM)


def pick_kernel(
    served, target_rows, features, outgoing, own, index, own_index, held, rows, picked, picked_own, sems, out_sems
):
    peers, _, capacity = served.shape
    loads = features.shape[0] // ROWS_AT_ONCE
    chunks = features.shape[1] // LANES
    stores = out_sems.shape[0] - 1
    span = peers // stores

    def load(step):
        part = pl.ds(step * ROWS_AT_ONCE, ROWS_AT_ONCE)
        return pltpu.make_async_copy(features.at[part], held.at[part], sems.at[step])

    lists = [
        pltpu.make_async_copy(served, index, sems.at[loads]),
        pltpu.make_async_copy(target_rows, own_index, sems.at[loads + 1]),
    ]
    for step in range(loads):
        load(step).start()
    for copy in lists:
        copy.start()
    for step in range(loads):
        load(step).wait()
        part = pl.ds(step * ROWS_AT_ONCE, ROWS_AT_ONCE)
        rows[part] = pltpu.einshape("n(cl)->ncl", held[part, :], c=chunks)
    for copy in lists:
        copy.wait()
    copies = []
    for step in range(stores):

        def some_peers(group, carry):
            for peer in range(PEERS_AT_ONCE):
                for slot in range(capacity):
                    p = group * PEERS_AT_ONCE + peer
                    picked[p * capacity + slot] = rows[index[p, 0, slot]]
            return carry

        groups = span // PEERS_AT_ONCE
        lax.fori_loop(step * groups, (step + 1) * groups, some_peers, 0)
        part = pl.ds(step * span * capacity, span * capacity)
        copies.append(pltpu.make_async_copy(picked.at[part], outgoing.at[part], out_sems.at[step]))
        copies[-1].start()

    def target(t, carry):
        picked_own[t] = rows[own_index[t]]
        return carry

    lax.fori_loop(0, own.shape[0], target, 0)
    copies.append(pltpu.make_async_copy(picked_own, own, out_sems.at[stores]))
    copies[-1].start()
    for copy in copies:
        copy.wait()


def pick(served, target_rows, features):
    peers, _, capacity = served.shape
    count, width = features.shape
    tile = (width // LANES, LANES)
    targets = target_rows.shape[0]
    hbm = pl.BlockSpec(memory_space=pltpu.HBM)
    anywhere = pl.BlockSpec(memory_space=pl.ANY)
    return pl.pallas_call(
        pick_kernel,
        out_shape=(
            pltpu.HBM((peers * capacity,) + tile, features.dtype),
            pltpu.HBM((targets,) + tile, features.dtype),
        ),
        in_specs=[anywhere, anywhere, hbm],
        out_specs=(hbm, hbm),
        scratch_shapes=[
            pltpu.SMEM(served.shape, jnp.int32),
            pltpu.SMEM(target_rows.shape, jnp.int32),
            pltpu.VMEM((count, width), features.dtype),
            pltpu.VMEM((count,) + tile, features.dtype),
            pltpu.VMEM((peers * capacity,) + tile, features.dtype),
            pltpu.VMEM((targets,) + tile, features.dtype),
            pltpu.SemaphoreType.DMA((count // ROWS_AT_ONCE + 2,)),
            pltpu.SemaphoreType.DMA((9,)),
        ],
        compiler_params=GRANT,
        cost_estimate=takes(COST_PICK),
        name="pick",
    )(served, in_hbm(target_rows), in_hbm(features))


def prepare_kernel(
    blocks, own, shares, output_weight, output_bias, *rest,
):
    mine, other = rest[:4], rest[4:8]
    hidden_weight, base, parts, total = rest[8:12]
    whole, spread, own_rows, held, held_base, held_parts, held_total, sems = rest[12:]
    targets, chunks, _ = own.shape
    half, side = mine[0].shape[2:]
    first_rows = pltpu.make_async_copy(output_weight.at[pl.ds(0, held.shape[0])], held, sems.at[32])
    first_rows.start()
    copies = []
    for far, pieces in enumerate((mine, other)):
        for second, piece in enumerate(pieces):
            for first in range(piece.shape[0]):
                at = 16 * far + 4 * second + first
                rows = pl.ds(pl.multiple_of(blocks[0, at] * half, half), half)
                columns = pl.ds(pl.multiple_of(blocks[1, at] * side, side), side)
                copies.append(
                    pltpu.make_async_copy(piece.at[first, 0], whole.at[rows, columns], sems.at[at])
                )
    for copy in copies:
        copy.start()

    spread[pl.ds(0, targets * chunks), :] = own[...].astype(jnp.float32).reshape(targets * chunks, LANES)
    for chunk in range(chunks):
        part = spread[pl.ds(chunk, targets, stride=chunks), :]
        own_rows[:, pl.ds(chunk * LANES, LANES)] = part.astype(jnp.bfloat16)
    share = shares[...]
    high = jnp.floor(share * (1.0 / 64.0))
    low = share - high * 64.0
    held_parts[...] = jnp.concatenate([high, low], axis=0).astype(jnp.bfloat16)
    held_total[...] = jnp.broadcast_to(jnp.sum(share, axis=1, keepdims=True), held_total.shape)
    first_rows.wait()
    held_base[...] = jnp.dot(own_rows[...], held[...], preferred_element_type=jnp.float32) + output_bias[...]
    for copy in copies:
        copy.wait()
    results = ((whole, hidden_weight), (held_base, base), (held_parts, parts), (held_total, total))
    stores = [pltpu.make_async_copy(held, out, sems.at[33 + at]) for at, (held, out) in enumerate(results)]
    for store in stores:
        store.start()
    for store in stores:
        store.wait()


def prepare(blocks, own, shares, output_weight, output_bias, mine, other):
    targets, chunks, _ = own.shape
    width = chunks * LANES
    units = output_weight.shape[1]
    hidden = output_weight.shape[0] - width
    vmem = pl.BlockSpec(memory_space=pltpu.VMEM)
    hbm = pl.BlockSpec(memory_space=pltpu.HBM)
    return pl.pallas_call(
        prepare_kernel,
        out_shape=(
            pltpu.HBM((width, hidden), jnp.bfloat16),
            pltpu.HBM((targets, units), jnp.float32),
            pltpu.HBM((2 * targets, LIVE), jnp.bfloat16),
            pltpu.HBM((targets, LANES), jnp.float32),
        ),
        in_specs=[pl.BlockSpec(memory_space=pltpu.SMEM), vmem, vmem, hbm, vmem] + [hbm] * 8,
        out_specs=(hbm,) * 4,
        scratch_shapes=[
            pltpu.VMEM((width, hidden), jnp.bfloat16),
            pltpu.VMEM((targets * chunks + chunks, LANES), jnp.float32),
            pltpu.VMEM((targets, width), jnp.bfloat16),
            pltpu.VMEM((width, units), jnp.bfloat16),
            pltpu.VMEM((targets, units), jnp.float32),
            pltpu.VMEM((2 * targets, LIVE), jnp.bfloat16),
            pltpu.VMEM((targets, LANES), jnp.float32),
            pltpu.SemaphoreType.DMA((37,)),
        ],
        compiler_params=GRANT,
        cost_estimate=takes(COST_PREPARE),
        name="prepare",
    )(
        blocks, own, shares, in_hbm(output_weight), output_bias.reshape(1, -1),
        *[in_hbm(piece) for piece in mine + other],
    )


def finish_kernel(
    source_hbm, arrived, parts_hbm, total_hbm, base_hbm, hidden_bias_hbm, hidden_weight, output_weight,
    embedding, source, spread, live_rows, pooled, held_hidden, held_output, parts, total, base, hidden_bias, sems,
):
    chunks = arrived.shape[1]
    targets, hidden = pooled.shape
    blocks = hidden // BLOCK
    small = ((parts_hbm, parts), (total_hbm, total), (base_hbm, base), (hidden_bias_hbm, hidden_bias))
    slots = pltpu.make_async_copy(source_hbm, source, sems.at[blocks + 5])
    slots.start()
    rest = [pltpu.make_async_copy(x, held, sems.at[blocks + 1 + at]) for at, (x, held) in enumerate(small)]
    for load in rest:
        load.start()
    loads = []
    for block in range(blocks):
        columns = pl.ds(block * BLOCK, BLOCK)
        loads.append(
            pltpu.make_async_copy(hidden_weight.at[:, columns], held_hidden.at[:, columns], sems.at[block])
        )
        loads[-1].start()

    def group(g, carry):
        at = lax.rem(g, 2) * (GROUP * chunks)
        for row in range(GROUP):
            place = pl.multiple_of(at + row * chunks, chunks)
            spread[pl.ds(place, chunks), :] = arrived[source[g * GROUP + row]].astype(jnp.float32)
        rows = pl.ds(pl.multiple_of(g * GROUP, GROUP), GROUP)
        for chunk in range(chunks):
            part = spread[pl.ds(at + chunk, GROUP, stride=chunks), :]
            live_rows[rows, pl.ds(chunk * LANES, LANES)] = part.astype(jnp.bfloat16)
        return carry

    slots.wait()
    lax.fori_loop(0, LIVE // GROUP, group, 0)
    skipped = output_weight.shape[0] - hidden
    last_rows = pltpu.make_async_copy(output_weight.at[pl.ds(skipped, hidden)], held_output, sems.at[blocks])
    last_rows.start()
    for load in rest:
        load.wait()
    for block in range(blocks):
        columns = pl.ds(block * BLOCK, BLOCK)
        loads[block].wait()
        product = jnp.dot(live_rows[...], held_hidden[:, columns], preferred_element_type=jnp.float32)
        transformed = jnp.maximum(product + hidden_bias[:, columns], 0.0).astype(jnp.bfloat16)
        both = jnp.dot(parts[...], transformed, preferred_element_type=jnp.float32)
        summed = both[:targets] * 64.0 + both[targets:]
        pooled[:, columns] = (summed / total[:, :1]).astype(jnp.bfloat16)
    last_rows.wait()
    combined = base[...] + jnp.dot(pooled[...], held_output[...], preferred_element_type=jnp.float32)
    combined = jnp.maximum(combined, 0.0)
    scale = lax.rsqrt(jnp.mean(combined * combined, axis=1, keepdims=True) + 1e-06)
    embedding[...] = (combined * scale).astype(jnp.bfloat16)


def finish(source, arrived, parts, total, base, hidden_bias, hidden_weight, output_weight):
    chunks = arrived.shape[1]
    targets = base.shape[0]
    width, hidden = hidden_weight.shape
    units = output_weight.shape[1]
    vmem = pl.BlockSpec(memory_space=pltpu.VMEM)
    hbm = pl.BlockSpec(memory_space=pltpu.HBM)
    return pl.pallas_call(
        finish_kernel,
        out_shape=jax.ShapeDtypeStruct((targets, units), jnp.bfloat16),
        in_specs=[hbm, vmem] + [hbm] * 6,
        out_specs=vmem,
        scratch_shapes=[
            pltpu.SMEM(source.shape, jnp.int32),
            pltpu.VMEM((2 * GROUP * chunks + chunks, LANES), jnp.float32),
            pltpu.VMEM((LIVE, width), jnp.bfloat16),
            pltpu.VMEM((targets, hidden), jnp.bfloat16),
            pltpu.VMEM((width, hidden), jnp.bfloat16),
            pltpu.VMEM((hidden, units), jnp.bfloat16),
            pltpu.VMEM(parts.shape, jnp.bfloat16),
            pltpu.VMEM(total.shape, jnp.float32),
            pltpu.VMEM(base.shape, jnp.float32),
            pltpu.VMEM((1, hidden), jnp.float32),
            pltpu.SemaphoreType.DMA((hidden // BLOCK + 6,)),
        ],
        compiler_params=GRANT,
        name="finish",
    )(
        in_hbm(source), pltpu.with_memory_space_constraint(arrived, pltpu.VMEM), in_hbm(parts), in_hbm(total),
        in_hbm(base), in_hbm(hidden_bias.reshape(1, -1)), in_hbm(hidden_weight), in_hbm(output_weight),
    )


def plan(neighbour_slot, counts, peers, capacity):
    owner, slot = neighbour_slot // capacity, neighbour_slot % capacity
    same = owner[:, :, None] == jnp.arange(peers, dtype=jnp.int32)
    used = jnp.max(jnp.where(same, slot[:, :, None] + 1, 0), axis=(0, 1))
    before = jnp.arange(peers)[:, None] < jnp.arange(peers)[None, :]
    start = jnp.sum(jnp.where(before, used[:, None], 0), axis=0)
    place = jnp.sum(jnp.where(same, start, 0), axis=2) + slot
    live = jnp.arange(LIVE, dtype=jnp.int32)
    hit = place[:, :, None] == live
    shares = jnp.sum(jnp.where(hit, counts[:, :, None], 0), axis=1).astype(jnp.float32)
    within = (start <= live[:, None]) & (live[:, None] < start + used)
    first = jnp.arange(peers, dtype=jnp.int32) * capacity - start
    source = jnp.sum(jnp.where(within, first, 0), axis=1) + live
    return source, shares


def shifted(x, second, by):
    pairs = []
    for dom in range(8):
        for grp in range(16):
            row, column = grp // 4, grp % 4
            if (dom % 2 == 0) != second:
                row = (row + by) % 4
            else:
                column = (column + by) % 4
            pairs.append((dom * 16 + grp, dom * 16 + row * 4 + column))
    return lax.ppermute(x, AXES, pairs)


def join_kernel(*refs):
    weights, (out, held, sems) = refs[:-3], refs[-3:]
    half = out.shape[2]
    core = lax.rem(lax.axis_index("dom"), 2)
    rows = pl.ds(pl.multiple_of(core * half, half), half)
    copies = [pltpu.make_async_copy(x.at[rows], held.at[at, 0], sems.at[at]) for at, x in enumerate(weights)]
    for copy in copies:
        copy.start()
    for copy in copies:
        copy.wait()
    whole = pltpu.make_async_copy(held, out, sems.at[len(weights)])
    whole.start()
    whole.wait()


def join(weights):
    rows, columns = weights[0].shape
    return pl.pallas_call(
        join_kernel,
        out_shape=pltpu.HBM((len(weights), 1, rows // 2, columns), weights[0].dtype),
        in_specs=[pl.BlockSpec(memory_space=pl.ANY)] * len(weights),
        out_specs=pl.BlockSpec(memory_space=pltpu.HBM),
        scratch_shapes=[
            pltpu.VMEM((len(weights), 1, rows // 2, columns), weights[0].dtype),
            pltpu.SemaphoreType.DMA((len(weights) + 1,)),
        ],
        compiler_params=pltpu.CompilerParams(vmem_limit_bytes=4 * 2**20),
        cost_estimate=takes(1),
        name="join",
    )(in_hbm(weights[0]), *weights[1:])


def block_places(back):
    core = lax.axis_index("dom") % 2 + back[0]
    row, column = lax.axis_index("grp") // 4, lax.axis_index("grp") % 4
    rows, columns = (row - back) % 4, (column - back) % 4
    of_core0 = (rows[None, :] * 4 + columns[:, None]).reshape(-1)
    of_core1 = (rows[:, None] * 4 + columns[None, :]).reshape(-1)
    same, across = jnp.where(core == 0, of_core0, of_core1), jnp.where(core == 0, of_core1, of_core0)
    half = jnp.repeat(jnp.stack([core, 1 - core]), 16)
    return jnp.stack([half, jnp.concatenate([same, across])]).astype(jnp.int32)


def on_device(
    features,
    requests,
    target_rows,
    neighbour_slot,
    counts,
    hidden_weight,
    hidden_bias,
    output_weight,
    output_bias,
):
    _, peers, capacity = requests.shape
    served = lax.all_to_all(requests.reshape(peers, 1, capacity), AXES, split_axis=0, concat_axis=0, tiled=True)
    near = join([hidden_weight] + [shifted(hidden_weight, False, by) for by in SHIFTS[1:]])
    mine = [near] + [shifted(near, True, by) for by in SHIFTS[1:]]
    outgoing, own = pick(served, target_rows, features)
    tile = outgoing.shape[1:]
    blocks = outgoing.reshape(peers, capacity * tile[0], tile[1])
    arrived = lax.all_to_all(blocks, AXES, split_axis=0, concat_axis=0, tiled=True)
    back = jnp.array(SHIFTS, jnp.int32)
    mine, neighbour_slot, counts, back = lax.optimization_barrier((mine, neighbour_slot, counts, back))
    places = block_places(back)
    other = [lax.ppermute(part, "dom", [(dom, dom ^ 1) for dom in range(8)]) for part in mine]
    source, shares = plan(neighbour_slot, counts, peers, capacity)
    weight, base, parts, total = prepare(places, own, shares, output_weight, output_bias, mine, other)
    return finish(
        source, arrived.reshape((peers * capacity,) + tile), parts, total, base, hidden_bias, weight, output_weight
    )


def solution(mesh):
    placed = (
        P(AXES, None),
        P(AXES, None, None),
        P(AXES),
        P(AXES, None),
        P(AXES, None),
        P(None, "grp"),
        P(),
        P(),
        P(),
    )
    return jax.shard_map(on_device, mesh=mesh, in_specs=placed, out_specs=P(AXES, None), check_vma=False)
```

```python
import functools

import jax
import jax.numpy as jnp
from jax import lax
from jax.experimental import pallas as pl
from jax.experimental.pallas import tpu as pltpu
from jax.sharding import PartitionSpec as P

LIVE = 800
LANES = 128
ROWS_AT_ONCE = 256
BLOCK = 1024
GROUP = 32
PEERS_AT_ONCE = 4
COST_PICK, COST_PREPARE = 7, 18
AXES = ("dom", "grp")
SHIFTS = (0, 1, 3, 2)
GRANT = pltpu.CompilerParams(vmem_limit_bytes=32 * 2**20)


def takes(microseconds):
    return pl.CostEstimate(flops=int(microseconds * 1.15e9), bytes_accessed=1, transcendentals=0)


def in_hbm(x):
    return pltpu.with_memory_space_constraint(x, pltpu.HBM)


def pick_kernel(
    served, target_rows, features, outgoing, own, index, own_index, held, rows, picked, picked_own, sems, out_sems
):
    peers, _, capacity = served.shape
    loads = features.shape[0] // ROWS_AT_ONCE
    chunks = features.shape[1] // LANES
    stores = out_sems.shape[0] - 1
    span = peers // stores

    def load(step):
        part = pl.ds(step * ROWS_AT_ONCE, ROWS_AT_ONCE)
        return pltpu.make_async_copy(features.at[part], held.at[part], sems.at[step])

    lists = [
        pltpu.make_async_copy(served, index, sems.at[loads]),
        pltpu.make_async_copy(target_rows, own_index, sems.at[loads + 1]),
    ]
    for copy in lists:
        copy.start()
    for step in range(loads):
        load(step).start()
    for step in range(loads):
        load(step).wait()
        part = pl.ds(step * ROWS_AT_ONCE, ROWS_AT_ONCE)
        rows[part] = pltpu.einshape("n(cl)->ncl", held[part, :], c=chunks)
    for copy in lists:
        copy.wait()
    copies = []
    for step in range(stores):

        def some_peers(group, carry):
            for peer in range(PEERS_AT_ONCE):
                for slot in range(capacity):
                    p = group * PEERS_AT_ONCE + peer
                    picked[p * capacity + slot] = rows[index[p, 0, slot]]
            return carry

        groups = span // PEERS_AT_ONCE
        lax.fori_loop(step * groups, (step + 1) * groups, some_peers, 0)
        part = pl.ds(step * span * capacity, span * capacity)
        copies.append(pltpu.make_async_copy(picked.at[part], outgoing.at[part], out_sems.at[step]))
        copies[-1].start()

    def target(t, carry):
        picked_own[t] = rows[own_index[t]]
        return carry

    lax.fori_loop(0, own.shape[0], target, 0)
    copies.append(pltpu.make_async_copy(picked_own, own, out_sems.at[stores]))
    copies[-1].start()
    for copy in copies:
        copy.wait()


def pick(served, target_rows, features):
    peers, _, capacity = served.shape
    count, width = features.shape
    tile = (width // LANES, LANES)
    targets = target_rows.shape[0]
    hbm = pl.BlockSpec(memory_space=pltpu.HBM)
    anywhere = pl.BlockSpec(memory_space=pl.ANY)
    return pl.pallas_call(
        pick_kernel,
        out_shape=(
            pltpu.HBM((peers * capacity,) + tile, features.dtype),
            pltpu.HBM((targets,) + tile, features.dtype),
        ),
        in_specs=[anywhere, anywhere, hbm],
        out_specs=(hbm, hbm),
        scratch_shapes=[
            pltpu.SMEM(served.shape, jnp.int32),
            pltpu.SMEM(target_rows.shape, jnp.int32),
            pltpu.VMEM((count, width), features.dtype),
            pltpu.VMEM((count,) + tile, features.dtype),
            pltpu.VMEM((peers * capacity,) + tile, features.dtype),
            pltpu.VMEM((targets,) + tile, features.dtype),
            pltpu.SemaphoreType.DMA((count // ROWS_AT_ONCE + 2,)),
            pltpu.SemaphoreType.DMA((9,)),
        ],
        compiler_params=GRANT,
        cost_estimate=takes(COST_PICK),
        name="pick",
    )(served, in_hbm(target_rows), in_hbm(features))


def prepare_kernel(
    blocks, own, shares, output_weight, output_bias, *rest,
):
    mine, other = rest[:4], rest[4:8]
    hidden_weight, base, parts, total = rest[8:12]
    whole, spread, own_rows, held, held_base, held_parts, held_total, sems = rest[12:]
    targets, chunks, _ = own.shape
    half, side = mine[0].shape[2:]
    first_rows = pltpu.make_async_copy(output_weight.at[pl.ds(0, held.shape[0])], held, sems.at[32])
    first_rows.start()
    copies = []
    for far, pieces in enumerate((mine, other)):
        for second, piece in enumerate(pieces):
            for first in range(piece.shape[0]):
                at = 16 * far + 4 * second + first
                rows = pl.ds(pl.multiple_of(blocks[0, at] * half, half), half)
                columns = pl.ds(pl.multiple_of(blocks[1, at] * side, side), side)
                copies.append(
                    pltpu.make_async_copy(piece.at[first, 0], whole.at[rows, columns], sems.at[at])
                )
    for copy in copies:
        copy.start()

    spread[pl.ds(0, targets * chunks), :] = own[...].astype(jnp.float32).reshape(targets * chunks, LANES)
    for chunk in range(chunks):
        part = spread[pl.ds(chunk, targets, stride=chunks), :]
        own_rows[:, pl.ds(chunk * LANES, LANES)] = part.astype(jnp.bfloat16)
    share = shares[...]
    high = jnp.floor(share * (1.0 / 64.0))
    low = share - high * 64.0
    held_parts[...] = jnp.concatenate([high, low], axis=0).astype(jnp.bfloat16)
    held_total[...] = jnp.broadcast_to(jnp.sum(share, axis=1, keepdims=True), held_total.shape)
    first_rows.wait()
    held_base[...] = jnp.dot(own_rows[...], held[...], preferred_element_type=jnp.float32) + output_bias[...]
    for copy in copies:
        copy.wait()
    results = ((whole, hidden_weight), (held_base, base), (held_parts, parts), (held_total, total))
    stores = [pltpu.make_async_copy(held, out, sems.at[33 + at]) for at, (held, out) in enumerate(results)]
    for store in stores:
        store.start()
    for store in stores:
        store.wait()


def prepare(blocks, own, shares, output_weight, output_bias, mine, other):
    targets, chunks, _ = own.shape
    width = chunks * LANES
    units = output_weight.shape[1]
    hidden = output_weight.shape[0] - width
    vmem = pl.BlockSpec(memory_space=pltpu.VMEM)
    hbm = pl.BlockSpec(memory_space=pltpu.HBM)
    return pl.pallas_call(
        prepare_kernel,
        out_shape=(
            pltpu.HBM((width, hidden), jnp.bfloat16),
            pltpu.HBM((targets, units), jnp.float32),
            pltpu.HBM((2 * targets, LIVE), jnp.bfloat16),
            pltpu.HBM((targets, LANES), jnp.float32),
        ),
        in_specs=[pl.BlockSpec(memory_space=pltpu.SMEM), vmem, vmem, hbm, vmem] + [hbm] * 8,
        out_specs=(hbm,) * 4,
        scratch_shapes=[
            pltpu.VMEM((width, hidden), jnp.bfloat16),
            pltpu.VMEM((targets * chunks + chunks, LANES), jnp.float32),
            pltpu.VMEM((targets, width), jnp.bfloat16),
            pltpu.VMEM((width, units), jnp.bfloat16),
            pltpu.VMEM((targets, units), jnp.float32),
            pltpu.VMEM((2 * targets, LIVE), jnp.bfloat16),
            pltpu.VMEM((targets, LANES), jnp.float32),
            pltpu.SemaphoreType.DMA((37,)),
        ],
        compiler_params=GRANT,
        cost_estimate=takes(COST_PREPARE),
        name="prepare",
    )(
        blocks, own, shares, in_hbm(output_weight), output_bias.reshape(1, -1),
        *[in_hbm(piece) for piece in mine + other],
    )


def finish_kernel(
    source_hbm, arrived, parts_hbm, total_hbm, base_hbm, hidden_bias_hbm, hidden_weight, output_weight,
    embedding, source, spread, live_rows, pooled, held_hidden, held_output, parts, total, base, hidden_bias, sems,
):
    chunks = arrived.shape[1]
    targets, hidden = pooled.shape
    blocks = hidden // BLOCK
    small = ((parts_hbm, parts), (total_hbm, total), (base_hbm, base), (hidden_bias_hbm, hidden_bias))
    slots = pltpu.make_async_copy(source_hbm, source, sems.at[blocks + 5])
    slots.start()
    rest = [pltpu.make_async_copy(x, held, sems.at[blocks + 1 + at]) for at, (x, held) in enumerate(small)]
    for load in rest:
        load.start()
    loads = []
    for block in range(blocks):
        columns = pl.ds(block * BLOCK, BLOCK)
        loads.append(
            pltpu.make_async_copy(hidden_weight.at[:, columns], held_hidden.at[:, columns], sems.at[block])
        )
        loads[-1].start()

    def group(g, carry):
        at = lax.rem(g, 2) * (GROUP * chunks)
        for row in range(GROUP):
            place = pl.multiple_of(at + row * chunks, chunks)
            spread[pl.ds(place, chunks), :] = arrived[source[g * GROUP + row]].astype(jnp.float32)
        rows = pl.ds(pl.multiple_of(g * GROUP, GROUP), GROUP)
        for chunk in range(chunks):
            part = spread[pl.ds(at + chunk, GROUP, stride=chunks), :]
            live_rows[rows, pl.ds(chunk * LANES, LANES)] = part.astype(jnp.bfloat16)
        return carry

    slots.wait()
    lax.fori_loop(0, LIVE // GROUP, group, 0)
    skipped = output_weight.shape[0] - hidden
    last_rows = pltpu.make_async_copy(output_weight.at[pl.ds(skipped, hidden)], held_output, sems.at[blocks])
    last_rows.start()
    for load in rest:
        load.wait()
    for block in range(blocks):
        columns = pl.ds(block * BLOCK, BLOCK)
        loads[block].wait()
        product = jnp.dot(live_rows[...], held_hidden[:, columns], preferred_element_type=jnp.float32)
        transformed = jnp.maximum(product + hidden_bias[:, columns], 0.0).astype(jnp.bfloat16)
        both = jnp.dot(parts[...], transformed, preferred_element_type=jnp.float32)
        summed = both[:targets] * 64.0 + both[targets:]
        pooled[:, columns] = (summed / total[:, :1]).astype(jnp.bfloat16)
    last_rows.wait()
    combined = base[...] + jnp.dot(pooled[...], held_output[...], preferred_element_type=jnp.float32)
    combined = jnp.maximum(combined, 0.0)
    scale = lax.rsqrt(jnp.mean(combined * combined, axis=1, keepdims=True) + 1e-06)
    embedding[...] = (combined * scale).astype(jnp.bfloat16)


def finish(source, arrived, parts, total, base, hidden_bias, hidden_weight, output_weight):
    chunks = arrived.shape[1]
    targets = base.shape[0]
    width, hidden = hidden_weight.shape
    units = output_weight.shape[1]
    vmem = pl.BlockSpec(memory_space=pltpu.VMEM)
    hbm = pl.BlockSpec(memory_space=pltpu.HBM)
    return pl.pallas_call(
        finish_kernel,
        out_shape=jax.ShapeDtypeStruct((targets, units), jnp.bfloat16),
        in_specs=[hbm, vmem] + [hbm] * 6,
        out_specs=vmem,
        scratch_shapes=[
            pltpu.SMEM(source.shape, jnp.int32),
            pltpu.VMEM((2 * GROUP * chunks + chunks, LANES), jnp.float32),
            pltpu.VMEM((LIVE, width), jnp.bfloat16),
            pltpu.VMEM((targets, hidden), jnp.bfloat16),
            pltpu.VMEM((width, hidden), jnp.bfloat16),
            pltpu.VMEM((hidden, units), jnp.bfloat16),
            pltpu.VMEM(parts.shape, jnp.bfloat16),
            pltpu.VMEM(total.shape, jnp.float32),
            pltpu.VMEM(base.shape, jnp.float32),
            pltpu.VMEM((1, hidden), jnp.float32),
            pltpu.SemaphoreType.DMA((hidden // BLOCK + 6,)),
        ],
        compiler_params=GRANT,
        name="finish",
    )(
        in_hbm(source), pltpu.with_memory_space_constraint(arrived, pltpu.VMEM), in_hbm(parts), in_hbm(total),
        in_hbm(base), in_hbm(hidden_bias.reshape(1, -1)), in_hbm(hidden_weight), in_hbm(output_weight),
    )


def plan(neighbour_slot, counts, peers, capacity):
    owner, slot = neighbour_slot // capacity, neighbour_slot % capacity
    same = owner[:, :, None] == jnp.arange(peers, dtype=jnp.int32)
    used = jnp.max(jnp.where(same, slot[:, :, None] + 1, 0), axis=(0, 1))
    before = jnp.arange(peers)[:, None] < jnp.arange(peers)[None, :]
    start = jnp.sum(jnp.where(before, used[:, None], 0), axis=0)
    place = jnp.sum(jnp.where(same, start, 0), axis=2) + slot
    live = jnp.arange(LIVE, dtype=jnp.int32)
    hit = place[:, :, None] == live
    shares = jnp.sum(jnp.where(hit, counts[:, :, None], 0), axis=1).astype(jnp.float32)
    within = (start <= live[:, None]) & (live[:, None] < start + used)
    first = jnp.arange(peers, dtype=jnp.int32) * capacity - start
    source = jnp.sum(jnp.where(within, first, 0), axis=1) + live
    return source, shares


def shifted(x, second, by):
    pairs = []
    for dom in range(8):
        for grp in range(16):
            row, column = grp // 4, grp % 4
            if (dom % 2 == 0) != second:
                row = (row + by) % 4
            else:
                column = (column + by) % 4
            pairs.append((dom * 16 + grp, dom * 16 + row * 4 + column))
    return lax.ppermute(x, AXES, pairs)


def join_kernel(*refs):
    weights, (out, held, sems) = refs[:-3], refs[-3:]
    half = out.shape[2]
    core = lax.rem(lax.axis_index("dom"), 2)
    rows = pl.ds(pl.multiple_of(core * half, half), half)
    copies = [pltpu.make_async_copy(x.at[rows], held.at[at, 0], sems.at[at]) for at, x in enumerate(weights)]
    for copy in copies:
        copy.start()
    for copy in copies:
        copy.wait()
    whole = pltpu.make_async_copy(held, out, sems.at[len(weights)])
    whole.start()
    whole.wait()


def join(weights):
    rows, columns = weights[0].shape
    return pl.pallas_call(
        join_kernel,
        out_shape=pltpu.HBM((len(weights), 1, rows // 2, columns), weights[0].dtype),
        in_specs=[pl.BlockSpec(memory_space=pl.ANY)] * len(weights),
        out_specs=pl.BlockSpec(memory_space=pltpu.HBM),
        scratch_shapes=[
            pltpu.VMEM((len(weights), 1, rows // 2, columns), weights[0].dtype),
            pltpu.SemaphoreType.DMA((len(weights) + 1,)),
        ],
        compiler_params=pltpu.CompilerParams(vmem_limit_bytes=4 * 2**20),
        cost_estimate=takes(1),
        name="join",
    )(in_hbm(weights[0]), *weights[1:])


def block_places(back):
    core = lax.axis_index("dom") % 2 + back[0]
    row, column = lax.axis_index("grp") // 4, lax.axis_index("grp") % 4
    rows, columns = (row - back) % 4, (column - back) % 4
    of_core0 = (rows[None, :] * 4 + columns[:, None]).reshape(-1)
    of_core1 = (rows[:, None] * 4 + columns[None, :]).reshape(-1)
    same, across = jnp.where(core == 0, of_core0, of_core1), jnp.where(core == 0, of_core1, of_core0)
    half = jnp.repeat(jnp.stack([core, 1 - core]), 16)
    return jnp.stack([half, jnp.concatenate([same, across])]).astype(jnp.int32)


def on_device(
    features,
    requests,
    target_rows,
    neighbour_slot,
    counts,
    hidden_weight,
    hidden_bias,
    output_weight,
    output_bias,
):
    _, peers, capacity = requests.shape
    served = lax.all_to_all(requests.reshape(peers, 1, capacity), AXES, split_axis=0, concat_axis=0, tiled=True)
    near = join([hidden_weight] + [shifted(hidden_weight, False, by) for by in SHIFTS[1:]])
    mine = [near] + [shifted(near, True, by) for by in SHIFTS[1:]]
    outgoing, own = pick(served, target_rows, features)
    tile = outgoing.shape[1:]
    blocks = outgoing.reshape(peers, capacity * tile[0], tile[1])
    arrived = lax.all_to_all(blocks, AXES, split_axis=0, concat_axis=0, tiled=True)
    back = jnp.array(SHIFTS, jnp.int32)
    mine, neighbour_slot, counts, back = lax.optimization_barrier((mine, neighbour_slot, counts, back))
    places = block_places(back)
    other = [lax.ppermute(part, "dom", [(dom, dom ^ 1) for dom in range(8)]) for part in mine]
    source, shares = plan(neighbour_slot, counts, peers, capacity)
    weight, base, parts, total = prepare(places, own, shares, output_weight, output_bias, mine, other)
    return finish(
        source, arrived.reshape((peers * capacity,) + tile), parts, total, base, hidden_bias, weight, output_weight
    )


def solution(mesh):
    placed = (
        P(AXES, None),
        P(AXES, None, None),
        P(AXES),
        P(AXES, None),
        P(AXES, None),
        P(None, "grp"),
        P(),
        P(),
        P(),
    )
    return jax.shard_map(on_device, mesh=mesh, in_specs=placed, out_specs=P(AXES, None), check_vma=False)
```

```python
import functools

import jax
import jax.numpy as jnp
from jax import lax
from jax.experimental import pallas as pl
from jax.experimental.pallas import tpu as pltpu
from jax.sharding import PartitionSpec as P

LIVE = 800
LANES = 128
ROWS_AT_ONCE = 128
BLOCK = 1024
GROUP = 32
PEERS_AT_ONCE = 4
COST_PICK, COST_PREPARE = 7, 18
AXES = ("dom", "grp")
SHIFTS = (0, 1, 3, 2)
GRANT = pltpu.CompilerParams(vmem_limit_bytes=32 * 2**20)


def takes(microseconds):
    return pl.CostEstimate(flops=int(microseconds * 1.15e9), bytes_accessed=1, transcendentals=0)


def in_hbm(x):
    return pltpu.with_memory_space_constraint(x, pltpu.HBM)


def pick_kernel(
    served, target_rows, features, outgoing, own, index, own_index, held, rows, picked, picked_own, sems, out_sems
):
    peers, _, capacity = served.shape
    loads = features.shape[0] // ROWS_AT_ONCE
    chunks = features.shape[1] // LANES
    stores = out_sems.shape[0] - 1
    span = peers // stores

    def load(step):
        part = pl.ds(step * ROWS_AT_ONCE, ROWS_AT_ONCE)
        return pltpu.make_async_copy(features.at[part], held.at[part], sems.at[step])

    lists = [
        pltpu.make_async_copy(served, index, sems.at[loads]),
        pltpu.make_async_copy(target_rows, own_index, sems.at[loads + 1]),
    ]
    for copy in lists:
        copy.start()
    for step in range(loads):
        load(step).start()
    for step in range(loads):
        load(step).wait()
        part = pl.ds(step * ROWS_AT_ONCE, ROWS_AT_ONCE)
        rows[part] = pltpu.einshape("n(cl)->ncl", held[part, :], c=chunks)
    for copy in lists:
        copy.wait()
    copies = []
    for step in range(stores):

        def some_peers(group, carry):
            for peer in range(PEERS_AT_ONCE):
                for slot in range(capacity):
                    p = group * PEERS_AT_ONCE + peer
                    picked[p * capacity + slot] = rows[index[p, 0, slot]]
            return carry

        groups = span // PEERS_AT_ONCE
        lax.fori_loop(step * groups, (step + 1) * groups, some_peers, 0)
        part = pl.ds(step * span * capacity, span * capacity)
        copies.append(pltpu.make_async_copy(picked.at[part], outgoing.at[part], out_sems.at[step]))
        copies[-1].start()

    def target(t, carry):
        picked_own[t] = rows[own_index[t]]
        return carry

    lax.fori_loop(0, own.shape[0], target, 0)
    copies.append(pltpu.make_async_copy(picked_own, own, out_sems.at[stores]))
    copies[-1].start()
    for copy in copies:
        copy.wait()


def pick(served, target_rows, features):
    peers, _, capacity = served.shape
    count, width = features.shape
    tile = (width // LANES, LANES)
    targets = target_rows.shape[0]
    hbm = pl.BlockSpec(memory_space=pltpu.HBM)
    anywhere = pl.BlockSpec(memory_space=pl.ANY)
    return pl.pallas_call(
        pick_kernel,
        out_shape=(
            pltpu.HBM((peers * capacity,) + tile, features.dtype),
            pltpu.HBM((targets,) + tile, features.dtype),
        ),
        in_specs=[anywhere, anywhere, hbm],
        out_specs=(hbm, hbm),
        scratch_shapes=[
            pltpu.SMEM(served.shape, jnp.int32),
            pltpu.SMEM(target_rows.shape, jnp.int32),
            pltpu.VMEM((count, width), features.dtype),
            pltpu.VMEM((count,) + tile, features.dtype),
            pltpu.VMEM((peers * capacity,) + tile, features.dtype),
            pltpu.VMEM((targets,) + tile, features.dtype),
            pltpu.SemaphoreType.DMA((count // ROWS_AT_ONCE + 2,)),
            pltpu.SemaphoreType.DMA((17,)),
        ],
        compiler_params=GRANT,
        cost_estimate=takes(COST_PICK),
        name="pick",
    )(served, in_hbm(target_rows), in_hbm(features))


def prepare_kernel(
    blocks, own, shares, output_weight, output_bias, *rest,
):
    mine, other = rest[:4], rest[4:8]
    hidden_weight, base, parts, total = rest[8:12]
    whole, spread, own_rows, held, held_base, held_parts, held_total, sems = rest[12:]
    targets, chunks, _ = own.shape
    half, side = mine[0].shape[2:]
    first_rows = pltpu.make_async_copy(output_weight.at[pl.ds(0, held.shape[0])], held, sems.at[32])
    first_rows.start()
    copies = []
    for far, pieces in enumerate((mine, other)):
        for second, piece in enumerate(pieces):
            for first in range(piece.shape[0]):
                at = 16 * far + 4 * second + first
                rows = pl.ds(pl.multiple_of(blocks[0, at] * half, half), half)
                columns = pl.ds(pl.multiple_of(blocks[1, at] * side, side), side)
                copies.append(
                    pltpu.make_async_copy(piece.at[first, 0], whole.at[rows, columns], sems.at[at])
                )
    for copy in copies:
        copy.start()

    spread[pl.ds(0, targets * chunks), :] = own[...].astype(jnp.float32).reshape(targets * chunks, LANES)
    for chunk in range(chunks):
        part = spread[pl.ds(chunk, targets, stride=chunks), :]
        own_rows[:, pl.ds(chunk * LANES, LANES)] = part.astype(jnp.bfloat16)
    share = shares[...]
    high = jnp.floor(share * (1.0 / 64.0))
    low = share - high * 64.0
    held_parts[...] = jnp.concatenate([high, low], axis=0).astype(jnp.bfloat16)
    held_total[...] = jnp.broadcast_to(jnp.sum(share, axis=1, keepdims=True), held_total.shape)
    first_rows.wait()
    held_base[...] = jnp.dot(own_rows[...], held[...], preferred_element_type=jnp.float32) + output_bias[...]
    for copy in copies:
        copy.wait()
    results = ((whole, hidden_weight), (held_base, base), (held_parts, parts), (held_total, total))
    stores = [pltpu.make_async_copy(held, out, sems.at[33 + at]) for at, (held, out) in enumerate(results)]
    for store in stores:
        store.start()
    for store in stores:
        store.wait()


def prepare(blocks, own, shares, output_weight, output_bias, mine, other):
    targets, chunks, _ = own.shape
    width = chunks * LANES
    units = output_weight.shape[1]
    hidden = output_weight.shape[0] - width
    vmem = pl.BlockSpec(memory_space=pltpu.VMEM)
    hbm = pl.BlockSpec(memory_space=pltpu.HBM)
    return pl.pallas_call(
        prepare_kernel,
        out_shape=(
            pltpu.HBM((width, hidden), jnp.bfloat16),
            pltpu.HBM((targets, units), jnp.float32),
            pltpu.HBM((2 * targets, LIVE), jnp.bfloat16),
            pltpu.HBM((targets, LANES), jnp.float32),
        ),
        in_specs=[pl.BlockSpec(memory_space=pltpu.SMEM), vmem, vmem, hbm, vmem] + [hbm] * 8,
        out_specs=(hbm,) * 4,
        scratch_shapes=[
            pltpu.VMEM((width, hidden), jnp.bfloat16),
            pltpu.VMEM((targets * chunks + chunks, LANES), jnp.float32),
            pltpu.VMEM((targets, width), jnp.bfloat16),
            pltpu.VMEM((width, units), jnp.bfloat16),
            pltpu.VMEM((targets, units), jnp.float32),
            pltpu.VMEM((2 * targets, LIVE), jnp.bfloat16),
            pltpu.VMEM((targets, LANES), jnp.float32),
            pltpu.SemaphoreType.DMA((37,)),
        ],
        compiler_params=GRANT,
        cost_estimate=takes(COST_PREPARE),
        name="prepare",
    )(
        blocks, own, shares, in_hbm(output_weight), output_bias.reshape(1, -1),
        *[in_hbm(piece) for piece in mine + other],
    )


def finish_kernel(
    source_hbm, arrived, parts_hbm, total_hbm, base_hbm, hidden_bias_hbm, hidden_weight, output_weight,
    embedding, source, spread, live_rows, pooled, held_hidden, held_output, parts, total, base, hidden_bias, sems,
):
    chunks = arrived.shape[1]
    targets, hidden = pooled.shape
    blocks = hidden // BLOCK
    small = ((parts_hbm, parts), (total_hbm, total), (base_hbm, base), (hidden_bias_hbm, hidden_bias))
    slots = pltpu.make_async_copy(source_hbm, source, sems.at[blocks + 5])
    slots.start()
    rest = [pltpu.make_async_copy(x, held, sems.at[blocks + 1 + at]) for at, (x, held) in enumerate(small)]
    for load in rest:
        load.start()
    loads = []
    for block in range(blocks):
        columns = pl.ds(block * BLOCK, BLOCK)
        loads.append(
            pltpu.make_async_copy(hidden_weight.at[:, columns], held_hidden.at[:, columns], sems.at[block])
        )
        loads[-1].start()

    def group(g, carry):
        at = lax.rem(g, 2) * (GROUP * chunks)
        for row in range(GROUP):
            place = pl.multiple_of(at + row * chunks, chunks)
            spread[pl.ds(place, chunks), :] = arrived[source[g * GROUP + row]].astype(jnp.float32)
        rows = pl.ds(pl.multiple_of(g * GROUP, GROUP), GROUP)
        for chunk in range(chunks):
            part = spread[pl.ds(at + chunk, GROUP, stride=chunks), :]
            live_rows[rows, pl.ds(chunk * LANES, LANES)] = part.astype(jnp.bfloat16)
        return carry

    slots.wait()
    lax.fori_loop(0, LIVE // GROUP, group, 0)
    skipped = output_weight.shape[0] - hidden
    last_rows = pltpu.make_async_copy(output_weight.at[pl.ds(skipped, hidden)], held_output, sems.at[blocks])
    last_rows.start()
    for load in rest:
        load.wait()
    for block in range(blocks):
        columns = pl.ds(block * BLOCK, BLOCK)
        loads[block].wait()
        product = jnp.dot(live_rows[...], held_hidden[:, columns], preferred_element_type=jnp.float32)
        transformed = jnp.maximum(product + hidden_bias[:, columns], 0.0).astype(jnp.bfloat16)
        both = jnp.dot(parts[...], transformed, preferred_element_type=jnp.float32)
        summed = both[:targets] * 64.0 + both[targets:]
        pooled[:, columns] = (summed / total[:, :1]).astype(jnp.bfloat16)
    last_rows.wait()
    combined = base[...] + jnp.dot(pooled[...], held_output[...], preferred_element_type=jnp.float32)
    combined = jnp.maximum(combined, 0.0)
    scale = lax.rsqrt(jnp.mean(combined * combined, axis=1, keepdims=True) + 1e-06)
    embedding[...] = (combined * scale).astype(jnp.bfloat16)


def finish(source, arrived, parts, total, base, hidden_bias, hidden_weight, output_weight):
    chunks = arrived.shape[1]
    targets = base.shape[0]
    width, hidden = hidden_weight.shape
    units = output_weight.shape[1]
    vmem = pl.BlockSpec(memory_space=pltpu.VMEM)
    hbm = pl.BlockSpec(memory_space=pltpu.HBM)
    return pl.pallas_call(
        finish_kernel,
        out_shape=jax.ShapeDtypeStruct((targets, units), jnp.bfloat16),
        in_specs=[hbm, vmem] + [hbm] * 6,
        out_specs=vmem,
        scratch_shapes=[
            pltpu.SMEM(source.shape, jnp.int32),
            pltpu.VMEM((2 * GROUP * chunks + chunks, LANES), jnp.float32),
            pltpu.VMEM((LIVE, width), jnp.bfloat16),
            pltpu.VMEM((targets, hidden), jnp.bfloat16),
            pltpu.VMEM((width, hidden), jnp.bfloat16),
            pltpu.VMEM((hidden, units), jnp.bfloat16),
            pltpu.VMEM(parts.shape, jnp.bfloat16),
            pltpu.VMEM(total.shape, jnp.float32),
            pltpu.VMEM(base.shape, jnp.float32),
            pltpu.VMEM((1, hidden), jnp.float32),
            pltpu.SemaphoreType.DMA((hidden // BLOCK + 6,)),
        ],
        compiler_params=GRANT,
        name="finish",
    )(
        in_hbm(source), pltpu.with_memory_space_constraint(arrived, pltpu.VMEM), in_hbm(parts), in_hbm(total),
        in_hbm(base), in_hbm(hidden_bias.reshape(1, -1)), in_hbm(hidden_weight), in_hbm(output_weight),
    )


def plan(neighbour_slot, counts, peers, capacity):
    owner, slot = neighbour_slot // capacity, neighbour_slot % capacity
    same = owner[:, :, None] == jnp.arange(peers, dtype=jnp.int32)
    used = jnp.max(jnp.where(same, slot[:, :, None] + 1, 0), axis=(0, 1))
    before = jnp.arange(peers)[:, None] < jnp.arange(peers)[None, :]
    start = jnp.sum(jnp.where(before, used[:, None], 0), axis=0)
    place = jnp.sum(jnp.where(same, start, 0), axis=2) + slot
    live = jnp.arange(LIVE, dtype=jnp.int32)
    hit = place[:, :, None] == live
    shares = jnp.sum(jnp.where(hit, counts[:, :, None], 0), axis=1).astype(jnp.float32)
    within = (start <= live[:, None]) & (live[:, None] < start + used)
    first = jnp.arange(peers, dtype=jnp.int32) * capacity - start
    source = jnp.sum(jnp.where(within, first, 0), axis=1) + live
    return source, shares


def shifted(x, second, by):
    pairs = []
    for dom in range(8):
        for grp in range(16):
            row, column = grp // 4, grp % 4
            if (dom % 2 == 0) != second:
                row = (row + by) % 4
            else:
                column = (column + by) % 4
            pairs.append((dom * 16 + grp, dom * 16 + row * 4 + column))
    return lax.ppermute(x, AXES, pairs)


def join_kernel(*refs):
    weights, (out, held, sems) = refs[:-3], refs[-3:]
    half = out.shape[2]
    core = lax.rem(lax.axis_index("dom"), 2)
    rows = pl.ds(pl.multiple_of(core * half, half), half)
    copies = [pltpu.make_async_copy(x.at[rows], held.at[at, 0], sems.at[at]) for at, x in enumerate(weights)]
    for copy in copies:
        copy.start()
    for copy in copies:
        copy.wait()
    whole = pltpu.make_async_copy(held, out, sems.at[len(weights)])
    whole.start()
    whole.wait()


def join(weights):
    rows, columns = weights[0].shape
    return pl.pallas_call(
        join_kernel,
        out_shape=pltpu.HBM((len(weights), 1, rows // 2, columns), weights[0].dtype),
        in_specs=[pl.BlockSpec(memory_space=pl.ANY)] * len(weights),
        out_specs=pl.BlockSpec(memory_space=pltpu.HBM),
        scratch_shapes=[
            pltpu.VMEM((len(weights), 1, rows // 2, columns), weights[0].dtype),
            pltpu.SemaphoreType.DMA((len(weights) + 1,)),
        ],
        compiler_params=pltpu.CompilerParams(vmem_limit_bytes=4 * 2**20),
        cost_estimate=takes(1),
        name="join",
    )(in_hbm(weights[0]), *weights[1:])


def block_places(back):
    core = lax.axis_index("dom") % 2 + back[0]
    row, column = lax.axis_index("grp") // 4, lax.axis_index("grp") % 4
    rows, columns = (row - back) % 4, (column - back) % 4
    of_core0 = (rows[None, :] * 4 + columns[:, None]).reshape(-1)
    of_core1 = (rows[:, None] * 4 + columns[None, :]).reshape(-1)
    same, across = jnp.where(core == 0, of_core0, of_core1), jnp.where(core == 0, of_core1, of_core0)
    half = jnp.repeat(jnp.stack([core, 1 - core]), 16)
    return jnp.stack([half, jnp.concatenate([same, across])]).astype(jnp.int32)


def on_device(
    features,
    requests,
    target_rows,
    neighbour_slot,
    counts,
    hidden_weight,
    hidden_bias,
    output_weight,
    output_bias,
):
    _, peers, capacity = requests.shape
    served = lax.all_to_all(requests.reshape(peers, 1, capacity), AXES, split_axis=0, concat_axis=0, tiled=True)
    near = join([hidden_weight] + [shifted(hidden_weight, False, by) for by in SHIFTS[1:]])
    mine = [near] + [shifted(near, True, by) for by in SHIFTS[1:]]
    outgoing, own = pick(served, target_rows, features)
    tile = outgoing.shape[1:]
    blocks = outgoing.reshape(peers, capacity * tile[0], tile[1])
    arrived = lax.all_to_all(blocks, AXES, split_axis=0, concat_axis=0, tiled=True)
    back = jnp.array(SHIFTS, jnp.int32)
    mine, neighbour_slot, counts, back = lax.optimization_barrier((mine, neighbour_slot, counts, back))
    places = block_places(back)
    other = [lax.ppermute(part, "dom", [(dom, dom ^ 1) for dom in range(8)]) for part in mine]
    source, shares = plan(neighbour_slot, counts, peers, capacity)
    weight, base, parts, total = prepare(places, own, shares, output_weight, output_bias, mine, other)
    return finish(
        source, arrived.reshape((peers * capacity,) + tile), parts, total, base, hidden_bias, weight, output_weight
    )


def solution(mesh):
    placed = (
        P(AXES, None),
        P(AXES, None, None),
        P(AXES),
        P(AXES, None),
        P(AXES, None),
        P(None, "grp"),
        P(),
        P(),
        P(),
    )
    return jax.shard_map(on_device, mesh=mesh, in_specs=placed, out_specs=P(AXES, None), check_vma=False)
```
